32 devices in a mesh: fsdp: 16 (over z, y, core), dp: 2 (over x).
Axes of the slice: x: 2, y: 2, z: 4, core: 2. Of those that a mesh axis runs over, the one named last changes fastest.
Arguments:
- inputs: bfloat16 [4096, 8192], P(('fsdp', 'dp')), may hold values from -6 to 6
- grad_value: bfloat16 [4096, 512], P(('fsdp', 'dp')), may hold values from -2 to 2
- w_value: bfloat16 [8192, 512], P('fsdp'), may hold values from -0.0625 to 0.0625
- adapter_down: bfloat16 [16, 8192, 64], P('dp', 'fsdp'), may hold values from -0.19921875 to 0.19921875
- adapter_up: bfloat16 [16, 512, 64], P('dp', 'fsdp'), may hold values from -0.25 to 0.25
- tenant_ids: int32 [32], P(('fsdp', 'dp')), may hold values from 0 to 15, as said below
- slot_table: int32 [16], replicated, may hold values from 0 to 15, each once
Outputs:
- input_gradient_rows: bfloat16 [4096, 8192], P(('fsdp', 'dp'))
- grad_down: bfloat16 [16, 8192, 64], P('dp', 'fsdp')
- grad_up: bfloat16 [16, 512, 64], P('dp', 'fsdp')
The draws below stay inside these ranges and needn't reach their ends.
Inputs may be any that keep to these rules, and one draw needn't show every extreme that they name: `tenant_ids`: the adapter that every token of a block of 128 tokens uses; within each token group every adapter is used by at least one block. `slot_table`: a permutation of the adapters' slots.
All inputs are finite; a program needn't handle non-finite values.
Results may differ from the reference program's by a relative error of at most 0.017.
Values may be sent and summed in bfloat16 or wider, within the bound.
No kernel may reach another device: no remote copies, remote signals or barrier semaphores. Data moves between devices by JAX's collectives and lax.ppermute only.
A program may use at most 64 MiB of HBM per device.

```python
import jax
import jax.numpy as jnp
from jax import lax

D = 8192
KVW = 512
R = 64
BLOCK = 128
TOK_DEV = 128
ADAPTERS = 16
TOKENS = 4096
N_FSDP = 16
N_DP = 2


def draw_tenant_ids(key, part):
    per_dev = TOK_DEV // BLOCK
    group_len = N_FSDP * per_dev

    def one_group(group_key):
        key_one, key_two, key_three, key_four = jax.random.split(group_key, 4)
        position = jnp.arange(group_len, dtype=jnp.int32)
        draw_one = jax.random.randint(key_one, (group_len,), 0, ADAPTERS, dtype=jnp.int32)
        draw_two = jax.random.randint(key_two, (group_len,), 0, ADAPTERS, dtype=jnp.int32)
        ranked = jax.random.permutation(key_three, ADAPTERS).astype(jnp.int32)
        skewed = jnp.take(ranked, jnp.minimum(draw_one, draw_two)).astype(jnp.int32)
        values = jnp.where(position < ADAPTERS, position, skewed).astype(jnp.int32)
        return jax.random.permutation(key_four, values).astype(jnp.int32)
    groups = jax.vmap(one_group)(jax.random.split(key, N_DP))
    return groups.reshape(N_DP, N_FSDP, per_dev).transpose(1, 0, 2).reshape(-1).astype(jnp.int32)


def shard_levels(own_key, dims, cuts, smallest, high):
    def one(dim, parts):
        heights = jax.random.uniform(jax.random.fold_in(jax.random.fold_in(own_key, 6), dim), (parts,), jnp.float32, smallest / len(cuts), high / len(cuts))
        return jnp.repeat(jnp.exp(heights), dims[dim] // parts).reshape((-1,) + (1,) * (len(dims) - dim - 1))

    factor_of = one(*cuts[0])
    for cut in cuts[1:]:
        factor_of = factor_of * one(*cut)
    return factor_of


def noise(key, shape, deviation, bound, shards=(), kind=jnp.bfloat16):
    values = jax.random.normal(key, shape, jnp.float32) * deviation
    if len(shards) > 0:
        values = shard_levels(key, shape, shards, -0.22, 0.18) * values
    return jnp.clip(values, min=-bound, max=bound).astype(kind)


def setup_inputs(seed: int = 0) -> dict:
    arg_keys = jax.random.split(jax.random.key(seed), 8)
    inputs = noise(arg_keys[0], (TOKENS, D), 1.0, 6.0, ((0, 32),))
    grad_value = noise(arg_keys[1], (TOKENS, KVW), 0.25, 2.0, ((0, 32),))
    w_value = noise(arg_keys[2], (D, KVW), D ** -0.5, 0.0625, ((0, 16),))
    adapter_down = noise(arg_keys[3], (ADAPTERS, D, R), 0.03, 0.19921875, ((0, 2), (1, 16)))
    adapter_up = noise(arg_keys[4], (ADAPTERS, KVW, R), KVW ** -0.5, 0.25, ((0, 2), (1, 16)))
    tenant_ids = draw_tenant_ids(jax.random.fold_in(arg_keys[7], 71), 0)
    slot_table = jax.random.permutation(arg_keys[6], ADAPTERS).astype(jnp.int32)
    return dict(inputs=inputs, grad_value=grad_value, w_value=w_value, adapter_down=adapter_down, adapter_up=adapter_up, tenant_ids=tenant_ids, slot_table=slot_table)


adapter_scale_factor = 2.0


def group_terms(x_group, grad_group, slot_group, w_value, adapter_down, adapter_up):
    def one_block(operands):
        input_block_tile, gradient_block_tile, slot = operands
        down_projection_matrix = lax.dynamic_index_in_dim(adapter_down, slot, 0, keepdims=False)
        up_mat = lax.dynamic_index_in_dim(adapter_up, slot, 0, keepdims=False)
        frozen_weight_gradient = jnp.dot(gradient_block_tile, w_value.T, preferred_element_type=jnp.float32).astype(jnp.bfloat16)
        frozen_weight_gradient = lax.optimization_barrier(frozen_weight_gradient).astype(jnp.float32)
        hidden_activation = jnp.dot(gradient_block_tile, up_mat, preferred_element_type=jnp.float32).astype(jnp.bfloat16)
        inner_rank_product = jnp.dot(input_block_tile, down_projection_matrix, preferred_element_type=jnp.float32).astype(jnp.bfloat16)
        adapter_gradient = adapter_scale_factor * jnp.dot(hidden_activation, down_projection_matrix.T, preferred_element_type=jnp.float32)
        gradient_row_set = (frozen_weight_gradient + adapter_gradient).astype(jnp.bfloat16)
        partial_down_factor = (adapter_scale_factor * jnp.dot(input_block_tile.T, hidden_activation, preferred_element_type=jnp.float32)).astype(jnp.bfloat16)
        partial_up_factor = (adapter_scale_factor * jnp.dot(gradient_block_tile.T, inner_rank_product, preferred_element_type=jnp.float32)).astype(jnp.bfloat16)
        return gradient_row_set, partial_down_factor, partial_up_factor
    return lax.map(one_block, (x_group, grad_group, slot_group))


def reference(inputs, grad_value, w_value, adapter_down, adapter_up, tenant_ids, slot_table):
    per_dev = TOK_DEV // BLOCK
    slots = jnp.take(slot_table, tenant_ids).astype(jnp.int32).reshape(N_FSDP, N_DP, per_dev)
    x_view = inputs.reshape(N_FSDP, N_DP, per_dev, BLOCK, D)
    grad_view = grad_value.reshape(N_FSDP, N_DP, per_dev, BLOCK, KVW)
    total_down = jnp.zeros((ADAPTERS, D, R), jnp.float32)
    total_up = jnp.zeros((ADAPTERS, KVW, R), jnp.float32)
    pieces = []
    for group in range(N_DP):
        x_group = x_view[:, group].reshape(N_FSDP * per_dev, BLOCK, D)
        grad_group = grad_view[:, group].reshape(N_FSDP * per_dev, BLOCK, KVW)
        slot_group = slots[:, group].reshape(N_FSDP * per_dev)
        gradient_row_set, partial_down_factor, partial_up_factor = group_terms(x_group, grad_group, slot_group, w_value, adapter_down, adapter_up)
        table_down = jax.ops.segment_sum(partial_down_factor.astype(jnp.float32), slot_group, num_segments=ADAPTERS).astype(jnp.bfloat16)
        table_up = jax.ops.segment_sum(partial_up_factor.astype(jnp.float32), slot_group, num_segments=ADAPTERS).astype(jnp.bfloat16)
        table_down, table_up = lax.optimization_barrier((table_down, table_up))
        total_down = total_down + table_down.astype(jnp.float32)
        total_up = total_up + table_up.astype(jnp.float32)
        pieces.append(gradient_row_set.reshape(N_FSDP, per_dev * BLOCK, D))
    input_gradient_rows = jnp.stack(pieces, axis=1).reshape(TOKENS, D)
    return input_gradient_rows, total_down.astype(jnp.bfloat16), total_up.astype(jnp.bfloat16)
```

```python
import functools

import jax
import jax.numpy as jnp
from jax import lax
from jax.experimental import pallas as pl
from jax.experimental.pallas import tpu as pltpu
from jax.sharding import PartitionSpec as P

adapter_scale_factor = 2.0
lanes = 128
BF16, F32 = jnp.bfloat16, jnp.float32
NT = (((1,), (1,)), ((), ()))
TN = (((0,), (0,)), ((), ()))
NN = (((1,), (0,)), ((), ()))


def params():
    return pltpu.CompilerParams(vmem_limit_bytes=40 * 1024 * 1024)


def cost(flops, nbytes):
    return pl.CostEstimate(flops=flops, bytes_accessed=nbytes, transcendentals=0)


def dot(a, b, dims):
    return lax.dot_general(a, b, dims, preferred_element_type=F32)


def packed_rows(kv_rows):
    if kv_rows % 32 == 0:
        return kv_rows // 2, 2
    return -(-kv_rows // 16) * 16, 1


def pack_up(block):
    kv_rows, rank = block.shape
    rows, groups = packed_rows(kv_rows)
    if groups == 2:
        return jnp.concatenate([block[:rows], block[rows:]], axis=1)
    block = jnp.concatenate([block, jnp.zeros((kv_rows, lanes - rank), block.dtype)], axis=1)
    if rows == kv_rows:
        return block
    return jnp.concatenate([block, jnp.zeros((rows - kv_rows, lanes), block.dtype)], axis=0)


def unpack_up(packed, kv_rows, rank):
    rows, groups = packed_rows(kv_rows)
    if groups == 2:
        return jnp.concatenate([packed[:, :rank], packed[:, rank:]], axis=0)
    return packed[:kv_rows, :rank]


def wide(ref, index, first, count, rank):
    return jnp.concatenate(
        [
            ref[index, pl.ds(pl.multiple_of((first + j) * rank, 16), rank), :]
            for j in range(count)
        ],
        axis=1,
    )


def select_kernel(dp_count, ids, table, *refs):
    downs, ups, out = refs[:dp_count], refs[dp_count : 2 * dp_count], refs[-1]
    own, rank, rows = downs[0].shape
    here = lax.axis_index("dp")
    cut = rows // lanes * rank

    @pl.loop(0, out.shape[0])
    def _(k):
        slot = table[ids[k]]
        place = slot % own
        step = (slot // own) ^ here
        for j in range(dp_count):

            @pl.when(step == j)
            def _():
                for c in range(rows // lanes):
                    out[k, c * rank : (c + 1) * rank, :] = downs[j][
                        place, :, c * lanes : (c + 1) * lanes
                    ]
                out[k, cut:, :] = pack_up(ups[j][place])


def middle_kernel(kv_rows, rank, x, g, got, hidden_out, back):
    fsdp_count = got.shape[0]
    tiles = x.shape[1] // fsdp_count // lanes
    rows = tiles * lanes
    cut = tiles * rank
    up = jnp.concatenate(
        [unpack_up(got[f, cut:, :], kv_rows, rank) for f in range(fsdp_count)], axis=0
    )
    hidden = dot(g[...], up, NN).astype(BF16)
    hidden_out[...] = hidden
    inner = jnp.zeros((x.shape[0], rank), F32)
    for f in range(fsdp_count):
        x_part = x[:, f * rows : (f + 1) * rows]
        inner += dot(x_part, wide(got, f, 0, tiles, rank), NT)
        down = (adapter_scale_factor * dot(hidden, x_part, TN)).astype(BF16)
        for c in range(tiles):
            back[f, c * rank : (c + 1) * rank, :] = down[:, c * lanes : (c + 1) * lanes]
    part_up = (adapter_scale_factor * dot(g[...], inner.astype(BF16), TN)).astype(BF16)
    for f in range(fsdp_count):
        back[f, cut:, :] = pack_up(part_up[f * kv_rows : (f + 1) * kv_rows])


def base_kernel(g_counts, w_count, *refs):
    gs, ws = refs[: len(g_counts)], refs[len(g_counts) : len(g_counts) + w_count]
    outs = refs[len(g_counts) + w_count :]
    at = 0
    cols = ws[0].shape[0]
    for ref, count in zip(gs, g_counts):
        rows = ref.shape[0] // count
        for n in range(count):
            for k in range(w_count):
                outs[at][:, k * cols : (k + 1) * cols] = dot(
                    ref[n * rows : (n + 1) * rows, :], ws[k][...], NT
                ).astype(BF16)
            at += 1


def out_kernel(rels, layers, inner_count, split, rows, rank, hidden, got, *refs):
    pieces, out = refs[:-1], refs[-1]
    f_here = lax.axis_index("fsdp")
    d_here = lax.axis_index("dp") % split
    cols = rows // split
    tiles = cols // lanes
    h = hidden[...]
    for (i_rel, d_rel), piece in zip(rels, pieces):
        d = d_here ^ d_rel
        for k in range(layers):
            f = f_here ^ (k * inner_count + i_rel)
            adapter = wide(got, f, d * tiles, tiles, rank)
            low = adapter_scale_factor * dot(h, adapter, NN)
            start = pl.multiple_of(f * rows + d * cols, lanes)
            out[:, pl.ds(start, cols)] = (
                piece[:, k * cols : (k + 1) * cols].astype(F32) + low
            ).astype(BF16)


def sort_kernel(dp_count, own, ids, table, got, *sends):
    here = lax.axis_index("dp")

    @pl.loop(0, got.shape[0])
    def _(k):
        slot = table[ids[k]]
        place = slot % own
        step = (slot // own) ^ here
        for j in range(1, dp_count):

            @pl.when(step == j)
            def _():
                sends[j - 1][place] = got[k]


def sum_kernel(dp_count, kv_rows, ids, table, got, *refs):
    received, (down, up) = refs[: dp_count - 1], refs[dp_count - 1 :]
    own, rank, rows = down.shape
    here = lax.axis_index("dp")
    tiles = rows // lanes

    @pl.loop(0, got.shape[0])
    def _(k):
        slot = table[ids[k]]
        place = slot % own

        @pl.when(slot // own == here)
        def _():
            total = got[k].astype(F32)
            for ref in received:
                total += ref[place].astype(F32)
            total = total.astype(BF16)
            for c in range(tiles):
                down[place, :, c * lanes : (c + 1) * lanes] = total[c * rank : (c + 1) * rank]
            up[place] = unpack_up(total[tiles * rank :], kv_rows, rank)


def vmem(count):
    return [pl.BlockSpec(memory_space=pltpu.VMEM)] * count


def smem(count):
    return [pl.BlockSpec(memory_space=pltpu.SMEM)] * count


def xor_pairs(count, bits):
    return [(n, n ^ bits) for n in range(count)]


def on_device(inputs, grad_value, w_value, adapter_down, adapter_up, tenant_ids, slot_table):
    tokens, width = inputs.shape
    kv_width = grad_value.shape[1]
    own, rows, rank = adapter_down.shape
    kv_rows = adapter_up.shape[1]
    fsdp_count = lax.axis_size("fsdp")
    dp_count = lax.axis_size("dp")
    inner_count = 1
    while inner_count * inner_count < fsdp_count:
        inner_count *= 2
    layers = fsdp_count // inner_count
    split = 1
    while split * 2 <= dp_count and rows // (split * 2) >= lanes:
        split *= 2
    cols = rows // split
    tall = rows // lanes * rank + packed_rows(kv_rows)[0]

    down_t = adapter_down.transpose(0, 2, 1)
    downs, ups = [down_t], [adapter_up]
    for j in range(1, dp_count):
        downs.append(lax.ppermute(down_t, "dp", xor_pairs(dp_count, j)))
        ups.append(lax.ppermute(adapter_up, "dp", xor_pairs(dp_count, j)))
    ids = lax.all_to_all(
        jnp.broadcast_to(tenant_ids[:, None], (fsdp_count, 1)), "fsdp", 0, 0, tiled=True
    ).reshape(-1)

    w_here = lax.dynamic_slice_in_dim(w_value, lax.axis_index("dp") % split * cols, cols, 0)
    ws = [w_here] + [
        lax.ppermute(w_here, "fsdp", xor_pairs(fsdp_count, k * inner_count))
        for k in range(1, layers)
    ]
    gs, g_counts, rels = [grad_value], [1], [(0, 0)]
    held = grad_value
    bit = 1
    while bit < split:
        new = lax.ppermute(held, "dp", xor_pairs(dp_count, bit))
        gs, g_counts = gs + [new], g_counts + [len(rels)]
        rels = rels + [(i, d | bit) for i, d in rels]
        held = jnp.concatenate([held, new], axis=0)
        bit *= 2
    bit = inner_count // 2
    while bit >= 1:
        new = lax.ppermute(held, "fsdp", xor_pairs(fsdp_count, bit))
        gs, g_counts = gs + [new], g_counts + [len(rels)]
        rels = rels + [(i | bit, d) for i, d in rels]
        bit //= 2
        if bit >= 1:
            held = jnp.concatenate([held, new], axis=0)
    piece = jax.ShapeDtypeStruct((tokens, layers * cols), BF16)
    pieces = pl.pallas_call(
        functools.partial(base_kernel, g_counts, layers),
        out_shape=[piece] * len(rels),
        in_specs=vmem(len(gs) + layers),
        out_specs=vmem(len(rels)),
        compiler_params=params(),
        cost_estimate=cost(2 * tokens * width * kv_width, 4 * tokens * width),
        name="base",
    )(*gs, *ws)
    total = fsdp_count * dp_count
    pieces = [pieces[0]] + [
        lax.ppermute(p, ("fsdp", "dp"), xor_pairs(total, i * dp_count + d))
        for (i, d), p in zip(rels[1:], pieces[1:])
    ]

    box = jax.ShapeDtypeStruct((fsdp_count, tall, lanes), BF16)
    box_bytes = 2 * fsdp_count * tall * lanes
    sent = pl.pallas_call(
        functools.partial(select_kernel, dp_count),
        out_shape=box,
        in_specs=smem(2) + vmem(2 * dp_count),
        out_specs=pl.BlockSpec(memory_space=pltpu.VMEM),
        compiler_params=params(),
        cost_estimate=cost(0, 2 * box_bytes),
        name="select",
    )(ids, slot_table, *downs, *ups)
    got = lax.all_to_all(sent, "fsdp", 0, 0, tiled=True)

    hidden, back = pl.pallas_call(
        functools.partial(middle_kernel, kv_rows, rank),
        out_shape=[jax.ShapeDtypeStruct((tokens, rank), BF16), box],
        in_specs=vmem(3),
        out_specs=vmem(2),
        compiler_params=params(),
        cost_estimate=cost(4 * tokens * width * rank, 2 * tokens * width + 2 * box_bytes),
        name="middle",
    )(inputs, grad_value, got)
    returned = lax.all_to_all(back, "fsdp", 0, 0, tiled=True)

    input_gradient_rows = pl.pallas_call(
        functools.partial(out_kernel, rels, layers, inner_count, split, rows, rank),
        out_shape=jax.ShapeDtypeStruct((tokens, width), BF16),
        in_specs=vmem(2 + len(rels)),
        out_specs=pl.BlockSpec(memory_space=pltpu.VMEM),
        compiler_params=params(),
        cost_estimate=cost(2 * tokens * width * rank, 4 * tokens * width + box_bytes),
        name="rows",
    )(hidden, got, *pieces)

    sends = pl.pallas_call(
        functools.partial(sort_kernel, dp_count, own),
        out_shape=[jax.ShapeDtypeStruct((own, tall, lanes), BF16)] * (dp_count - 1),
        in_specs=smem(2) + vmem(1),
        out_specs=vmem(dp_count - 1),
        compiler_params=params(),
        cost_estimate=cost(0, 2 * box_bytes),
        name="sort",
    )(ids, slot_table, returned)
    received = [
        lax.ppermute(s, "dp", xor_pairs(dp_count, j + 1)) for j, s in enumerate(sends)
    ]
    grad_down_t, grad_up = pl.pallas_call(
        functools.partial(sum_kernel, dp_count, kv_rows),
        out_shape=[
            jax.ShapeDtypeStruct((own, rank, rows), BF16),
            jax.ShapeDtypeStruct(adapter_up.shape, BF16),
        ],
        in_specs=smem(2) + vmem(dp_count),
        out_specs=vmem(2),
        compiler_params=params(),
        cost_estimate=cost(0, 2 * box_bytes),
        name="sums",
    )(ids, slot_table, returned, *received)
    return (input_gradient_rows, grad_down_t.transpose(0, 2, 1), grad_up)


def solution(mesh):
    in_specs = (
        P(("fsdp", "dp"), None),
        P(("fsdp", "dp"), None),
        P("fsdp", None),
        P("dp", "fsdp", None),
        P("dp", "fsdp", None),
        P(("fsdp", "dp")),
        P(),
    )
    out_specs = (P(("fsdp", "dp"), None), P("dp", "fsdp", None), P("dp", "fsdp", None))
    return jax.shard_map(
        on_device, mesh=mesh, in_specs=in_specs, out_specs=out_specs, check_vma=False
    )
```

```python
import functools
import math

import jax
import jax.numpy as jnp
from jax import lax
from jax.experimental import pallas as pl
from jax.experimental.pallas import tpu as pltpu
from jax.sharding import PartitionSpec as P

adapter_scale_factor = 2.0
lanes = 128
base_weight = 12
BF16, F32 = jnp.bfloat16, jnp.float32
NT = (((1,), (1,)), ((), ()))
TN = (((0,), (0,)), ((), ()))
NN = (((1,), (0,)), ((), ()))


def params():
    return pltpu.CompilerParams(vmem_limit_bytes=40 * 1024 * 1024)


def cost(flops, nbytes):
    return pl.CostEstimate(flops=flops, bytes_accessed=nbytes, transcendentals=0)


def dot(a, b, dims):
    return lax.dot_general(a, b, dims, preferred_element_type=F32)


def packed_rows(kv_rows):
    if kv_rows % 32 == 0:
        return kv_rows // 2, 2
    return -(-kv_rows // 16) * 16, 1


def pack_up(block):
    kv_rows, rank = block.shape
    rows, groups = packed_rows(kv_rows)
    if groups == 2:
        return jnp.concatenate([block[:rows], block[rows:]], axis=1)
    block = jnp.concatenate([block, jnp.zeros((kv_rows, lanes - rank), block.dtype)], axis=1)
    if rows == kv_rows:
        return block
    return jnp.concatenate([block, jnp.zeros((rows - kv_rows, lanes), block.dtype)], axis=0)


def unpack_up(packed, kv_rows, rank):
    rows, groups = packed_rows(kv_rows)
    if groups == 2:
        return jnp.concatenate([packed[:, :rank], packed[:, rank:]], axis=0)
    return packed[:kv_rows, :rank]


def wide(ref, index, first, count, rank):
    return jnp.concatenate(
        [
            ref[index, pl.ds(pl.multiple_of((first + j) * rank, 16), rank), :]
            for j in range(count)
        ],
        axis=1,
    )


def select_kernel(dp_count, ids, table, *refs):
    downs, ups, out = refs[:dp_count], refs[dp_count : 2 * dp_count], refs[-1]
    own, rank, rows = downs[0].shape
    here = lax.axis_index("dp")
    cut = rows // lanes * rank

    @pl.loop(0, out.shape[0])
    def _(k):
        slot = table[ids[k]]
        place = slot % own
        step = (slot // own) ^ here
        for j in range(dp_count):

            @pl.when(step == j)
            def _():
                for c in range(rows // lanes):
                    out[k, c * rank : (c + 1) * rank, :] = downs[j][
                        place, :, c * lanes : (c + 1) * lanes
                    ]
                out[k, cut:, :] = pack_up(ups[j][place])


def middle_kernel(kv_rows, rank, x, g, got, hidden_out, back):
    fsdp_count = got.shape[0]
    tiles = x.shape[1] // fsdp_count // lanes
    rows = tiles * lanes
    cut = tiles * rank
    up = jnp.concatenate(
        [unpack_up(got[f, cut:, :], kv_rows, rank) for f in range(fsdp_count)], axis=0
    )
    hidden = dot(g[...], up, NN).astype(BF16)
    hidden_out[...] = hidden
    inner = jnp.zeros((x.shape[0], rank), F32)
    for f in range(fsdp_count):
        x_part = x[:, f * rows : (f + 1) * rows]
        inner += dot(x_part, wide(got, f, 0, tiles, rank), NT)
        down = (adapter_scale_factor * dot(hidden, x_part, TN)).astype(BF16)
        for c in range(tiles):
            back[f, c * rank : (c + 1) * rank, :] = down[:, c * lanes : (c + 1) * lanes]
    part_up = (adapter_scale_factor * dot(g[...], inner.astype(BF16), TN)).astype(BF16)
    for f in range(fsdp_count):
        back[f, cut:, :] = pack_up(part_up[f * kv_rows : (f + 1) * kv_rows])


def base_kernel(g_counts, w_count, *refs):
    gs, ws = refs[: len(g_counts)], refs[len(g_counts) : len(g_counts) + w_count]
    outs = refs[len(g_counts) + w_count :]
    at = 0
    cols = ws[0].shape[0]
    for ref, count in zip(gs, g_counts):
        rows = ref.shape[0] // count
        for n in range(count):
            for k in range(w_count):
                outs[at][:, k * cols : (k + 1) * cols] = dot(
                    ref[n * rows : (n + 1) * rows, :], ws[k][...], NT
                ).astype(BF16)
            at += 1


def out_kernel(rels, layers, inner_count, split, rows, rank, hidden, got, *refs):
    pieces, out = refs[:-1], refs[-1]
    f_here = lax.axis_index("fsdp")
    d_here = lax.axis_index("dp") % split
    cols = rows // split
    tiles = cols // lanes
    h = hidden[...]
    for (i_rel, d_rel), piece in zip(rels, pieces):
        d = d_here ^ d_rel
        for k in range(2 * layers):
            f = f_here ^ (k % layers * inner_count + k // layers + i_rel)
            adapter = wide(got, f, d * tiles, tiles, rank)
            low = adapter_scale_factor * dot(h, adapter, NN)
            start = pl.multiple_of(f * rows + d * cols, lanes)
            out[:, pl.ds(start, cols)] = (
                piece[:, k * cols : (k + 1) * cols].astype(F32) + low
            ).astype(BF16)


def sort_kernel(dp_count, own, ids, table, got, *sends):
    here = lax.axis_index("dp")

    @pl.loop(0, got.shape[0])
    def _(k):
        slot = table[ids[k]]
        place = slot % own
        step = (slot // own) ^ here
        for j in range(1, dp_count):

            @pl.when(step == j)
            def _():
                sends[j - 1][place] = got[k]


def sum_kernel(dp_count, kv_rows, ids, table, got, *refs):
    received, (down, up) = refs[: dp_count - 1], refs[dp_count - 1 :]
    own, rank, rows = down.shape
    here = lax.axis_index("dp")
    tiles = rows // lanes

    @pl.loop(0, got.shape[0])
    def _(k):
        slot = table[ids[k]]
        place = slot % own

        @pl.when(slot // own == here)
        def _():
            total = got[k].astype(F32)
            for ref in received:
                total += ref[place].astype(F32)
            total = total.astype(BF16)
            for c in range(tiles):
                down[place, :, c * lanes : (c + 1) * lanes] = total[c * rank : (c + 1) * rank]
            up[place] = unpack_up(total[tiles * rank :], kv_rows, rank)


def vmem(count):
    return [pl.BlockSpec(memory_space=pltpu.VMEM)] * count


def smem(count):
    return [pl.BlockSpec(memory_space=pltpu.SMEM)] * count


def bits(count):
    return [1 << n for n in range(count.bit_length() - 1)]


def axis_count(axis):
    names = (axis,) if isinstance(axis, str) else axis
    return math.prod(lax.axis_size(name) for name in names)


def exchange(name, array, axis, bits):
    with jax.named_scope(name):
        return lax.ppermute(array, axis, xor_pairs(axis_count(axis), bits))


def xor_pairs(count, bits):
    return [(n, n ^ bits) for n in range(count)]


def on_device(inputs, grad_value, w_value, adapter_down, adapter_up, tenant_ids, slot_table):
    tokens, width = inputs.shape
    kv_width = grad_value.shape[1]
    own, rows, rank = adapter_down.shape
    kv_rows = adapter_up.shape[1]
    fsdp_count = lax.axis_size("fsdp")
    dp_count = lax.axis_size("dp")
    inner_count = 1
    while inner_count * inner_count < fsdp_count:
        inner_count *= 2
    layers = fsdp_count // inner_count
    split = 1
    while split * 2 <= dp_count and rows // (split * 2) >= lanes:
        split *= 2
    cols = rows // split
    tall = rows // lanes * rank + packed_rows(kv_rows)[0]

    down_t = adapter_down.transpose(0, 2, 1)
    downs, ups = [down_t], [adapter_up]
    for j in range(1, dp_count):
        downs.append(exchange("down_dp", down_t, "dp", j))
        ups.append(exchange("up_dp", adapter_up, "dp", j))
    with jax.named_scope("ids"):
        ids = lax.all_to_all(
            jnp.broadcast_to(tenant_ids[:, None, None], (fsdp_count, 1, lanes)), "fsdp", 0, 0, tiled=True
        )[:, 0, 0]

    w_here = lax.dynamic_slice_in_dim(w_value, lax.axis_index("dp") % split * cols, cols, 0)
    ws = [w_here] + [None] * (layers - 1)
    for bit in bits(layers):
        ws[bit] = exchange("w_layers", w_here, "fsdp", bit * inner_count)
    gs, g_counts, rels, held = [grad_value], [1], [(0, 0)], grad_value
    stages = [("fsdp", bit) for bit in bits(inner_count)[1:]] + [("dp", bit) for bit in bits(split)]
    for n, (axis, bit) in enumerate(stages):
        new = exchange("g_" + axis, held, axis, bit)
        gs, g_counts = gs + [new], g_counts + [len(rels)]
        rels = rels + [(i | bit, d) if axis == "fsdp" else (i, d | bit) for i, d in rels]
        if n + 1 < len(stages):
            held = jnp.concatenate([held, new], axis=0)
    ids, downs, ups, gs, ws = lax.optimization_barrier((ids, downs, ups, gs, ws))

    box = jax.ShapeDtypeStruct((fsdp_count, tall, lanes), BF16)
    box_bytes = 2 * fsdp_count * tall * lanes
    sent = pl.pallas_call(
        functools.partial(select_kernel, dp_count),
        out_shape=box,
        in_specs=smem(2) + vmem(2 * dp_count),
        out_specs=pl.BlockSpec(memory_space=pltpu.VMEM),
        compiler_params=params(),
        cost_estimate=cost(0, 2 * box_bytes),
        name="select",
    )(ids, slot_table, *downs, *ups)
    with jax.named_scope("adapters_to_blocks"):
        got = lax.all_to_all(sent, "fsdp", 0, 0, tiled=True)
    for bit in reversed(bits(layers)):
        for k in range(0, layers, 2 * bit):
            if ws[k + bit] is None:
                ws[k + bit] = exchange("w_last", ws[k], "fsdp", bit * inner_count)
    ws = ws + [exchange("w_core", w, "fsdp", 1) for w in ws]

    pieces = pl.pallas_call(
        functools.partial(base_kernel, g_counts, len(ws)),
        out_shape=[jax.ShapeDtypeStruct((tokens, len(ws) * cols), BF16)] * len(rels),
        in_specs=vmem(len(gs) + len(ws)),
        out_specs=vmem(len(rels)),
        compiler_params=params(),
        cost_estimate=cost(
            base_weight * 2 * tokens * width * kv_width, base_weight * 4 * tokens * width
        ),
        name="base",
    )(*gs, *ws)
    pieces = [pieces[0]] + [
        exchange("pieces%d%d" % (i, d), p, ("fsdp", "dp"), i * dp_count + d)
        for (i, d), p in zip(rels[1:], pieces[1:])
    ]
    got, pieces[:-1] = lax.optimization_barrier((got, pieces[:-1]))

    hidden, back = pl.pallas_call(
        functools.partial(middle_kernel, kv_rows, rank),
        out_shape=[jax.ShapeDtypeStruct((tokens, rank), BF16), box],
        in_specs=vmem(3),
        out_specs=vmem(2),
        compiler_params=params(),
        cost_estimate=cost(4 * tokens * width * rank, 2 * tokens * width + 2 * box_bytes),
        name="middle",
    )(inputs, grad_value, got)
    with jax.named_scope("gradients_back"):
        returned = lax.all_to_all(back, "fsdp", 0, 0, tiled=True)
    returned, pieces = lax.optimization_barrier((returned, pieces))

    input_gradient_rows = pl.pallas_call(
        functools.partial(out_kernel, rels, layers, inner_count, split, rows, rank),
        out_shape=jax.ShapeDtypeStruct((tokens, width), BF16),
        in_specs=vmem(2 + len(rels)),
        out_specs=pl.BlockSpec(memory_space=pltpu.VMEM),
        compiler_params=params(),
        cost_estimate=cost(2 * tokens * width * rank, 4 * tokens * width + box_bytes),
        name="rows",
    )(hidden, got, *pieces)

    sends = pl.pallas_call(
        functools.partial(sort_kernel, dp_count, own),
        out_shape=[jax.ShapeDtypeStruct((own, tall, lanes), BF16)] * (dp_count - 1),
        in_specs=smem(2) + vmem(1),
        out_specs=vmem(dp_count - 1),
        compiler_params=params(),
        cost_estimate=cost(0, 2 * box_bytes),
        name="sort",
    )(ids, slot_table, returned)
    received = [
        exchange("grads_dp", s, "dp", j + 1) for j, s in enumerate(sends)
    ]
    received, input_gradient_rows = lax.optimization_barrier((received, input_gradient_rows))
    grad_down_t, grad_up = pl.pallas_call(
        functools.partial(sum_kernel, dp_count, kv_rows),
        out_shape=[
            jax.ShapeDtypeStruct((own, rank, rows), BF16),
            jax.ShapeDtypeStruct(adapter_up.shape, BF16),
        ],
        in_specs=smem(2) + vmem(dp_count),
        out_specs=vmem(2),
        compiler_params=params(),
        cost_estimate=cost(0, 2 * box_bytes),
        name="sums",
    )(ids, slot_table, returned, *received)
    return (input_gradient_rows, grad_down_t.transpose(0, 2, 1), grad_up)


def solution(mesh):
    in_specs = (
        P(("fsdp", "dp"), None),
        P(("fsdp", "dp"), None),
        P("fsdp", None),
        P("dp", "fsdp", None),
        P("dp", "fsdp", None),
        P(("fsdp", "dp")),
        P(),
    )
    out_specs = (P(("fsdp", "dp"), None), P("dp", "fsdp", None), P("dp", "fsdp", None))
    return jax.shard_map(
        on_device, mesh=mesh, in_specs=in_specs, out_specs=out_specs, check_vma=False
    )
```

```python
import functools
import math

import jax
import jax.numpy as jnp
from jax import lax
from jax.experimental import pallas as pl
from jax.experimental.pallas import tpu as pltpu
from jax.sharding import PartitionSpec as P

adapter_scale_factor = 2.0
lanes = 128
base_weight = 11
store_parts = 4
BF16, F32 = jnp.bfloat16, jnp.float32
NT = (((1,), (1,)), ((), ()))
TN = (((0,), (0,)), ((), ()))
NN = (((1,), (0,)), ((), ()))


def params():
    return pltpu.CompilerParams(vmem_limit_bytes=40 * 1024 * 1024)


def cost(flops, nbytes):
    return pl.CostEstimate(flops=flops, bytes_accessed=nbytes, transcendentals=0)


def dot(a, b, dims):
    return lax.dot_general(a, b, dims, preferred_element_type=F32)


def packed_rows(kv_rows):
    if kv_rows % 32 == 0:
        return kv_rows // 2, 2
    return -(-kv_rows // 16) * 16, 1


def pack_up(block):
    kv_rows, rank = block.shape
    rows, groups = packed_rows(kv_rows)
    if groups == 2:
        return jnp.concatenate([block[:rows], block[rows:]], axis=1)
    block = jnp.concatenate([block, jnp.zeros((kv_rows, lanes - rank), block.dtype)], axis=1)
    if rows == kv_rows:
        return block
    return jnp.concatenate([block, jnp.zeros((rows - kv_rows, lanes), block.dtype)], axis=0)


def unpack_up(packed, kv_rows, rank):
    rows, groups = packed_rows(kv_rows)
    if groups == 2:
        return jnp.concatenate([packed[:, :rank], packed[:, rank:]], axis=0)
    return packed[:kv_rows, :rank]


def wide(ref, index, first, count, rank):
    return jnp.concatenate(
        [
            ref[index, pl.ds(pl.multiple_of((first + j) * rank, 16), rank), :]
            for j in range(count)
        ],
        axis=1,
    )


def select_kernel(dp_count, ids, table, *refs):
    downs, ups, out = refs[:dp_count], refs[dp_count : 2 * dp_count], refs[-1]
    own, rank, rows = downs[0].shape
    here = lax.axis_index("dp")
    cut = rows // lanes * rank

    @pl.loop(0, out.shape[0])
    def _(k):
        slot = table[ids[k]]
        place = slot % own
        step = (slot // own) ^ here
        for j in range(dp_count):

            @pl.when(step == j)
            def _():
                for c in range(rows // lanes):
                    out[k, c * rank : (c + 1) * rank, :] = downs[j][
                        place, :, c * lanes : (c + 1) * lanes
                    ]
                out[k, cut:, :] = pack_up(ups[j][place])


def middle_kernel(kv_rows, rank, halves, x, g, got, hidden_out, back, out, up_out, sems):
    fsdp_count = got.shape[0]
    tiles = x.shape[1] // fsdp_count // lanes
    rows = tiles * lanes
    cut = tiles * rank
    up = jnp.concatenate(
        [unpack_up(got[f, cut:, :], kv_rows, rank) for f in range(fsdp_count)], axis=0
    )
    hidden = dot(g[...], up, NN).astype(BF16)
    hidden_out[...] = hidden
    inner = jnp.zeros((x.shape[0], rank), F32)
    stores = []
    step = max(1, fsdp_count // store_parts)
    for f in range(fsdp_count):
        x_part = x[:, f * rows : (f + 1) * rows]
        inner += dot(x_part, wide(got, f, 0, tiles, rank), NT)
        down = (adapter_scale_factor * dot(hidden, x_part, TN)).astype(BF16)
        for c in range(tiles):
            half, at = c * halves // tiles, c % (tiles // halves) * rank
            out[f * halves + half, at : at + rank, :] = down[:, c * lanes : (c + 1) * lanes]
        if (f + 1) % step == 0:
            here = pl.ds((f + 1 - step) * halves, step * halves)
            stores.append(
                pltpu.make_async_copy(
                    out.at[here], back.at[here, 0 : out.shape[1], :], sems.at[len(stores)]
                )
            )
            stores[-1].start()
    part_up = (adapter_scale_factor * dot(g[...], inner.astype(BF16), TN)).astype(BF16)
    for f in range(fsdp_count):
        packed = pack_up(part_up[f * kv_rows : (f + 1) * kv_rows])
        for half in range(halves):
            up_out[f * halves + half] = packed
    stores.append(
        pltpu.make_async_copy(
            up_out,
            back.at[:, out.shape[1] : out.shape[1] + up_out.shape[1], :],
            sems.at[len(stores)],
        )
    )
    stores[-1].start()
    for store in stores:
        store.wait()


def base_kernel(g_counts, w_count, *refs):
    gs, ws = refs[: len(g_counts)], refs[len(g_counts) : len(g_counts) + w_count]
    outs = refs[len(g_counts) + w_count :]
    at = 0
    cols = ws[0].shape[0]
    for ref, count in zip(gs, g_counts):
        rows = ref.shape[0] // count
        for n in range(count):
            for k in range(w_count):
                outs[at][:, k * cols : (k + 1) * cols] = dot(
                    ref[n * rows : (n + 1) * rows, :], ws[k][...], NT
                ).astype(BF16)
            at += 1


def out_kernel(rels, layers, inner_count, split, rows, rank, hidden, got, *refs):
    pieces, out = refs[:-1], refs[-1]
    f_here = lax.axis_index("fsdp")
    d_here = lax.axis_index("dp") % split
    cols = rows // split
    tiles = cols // lanes
    h = hidden[...]
    for (i_rel, d_rel), piece in zip(rels, pieces):
        d = d_here ^ d_rel
        for k in range(2 * layers):
            f = f_here ^ (k % layers * inner_count + k // layers + i_rel)
            adapter = wide(got, f, d * tiles, tiles, rank)
            low = adapter_scale_factor * dot(h, adapter, NN)
            start = pl.multiple_of(f * rows + d * cols, lanes)
            out[:, pl.ds(start, cols)] = (
                piece[:, k * cols : (k + 1) * cols].astype(F32) + low
            ).astype(BF16)


def sort_kernel(dp_count, own, ids, table, got, *sends):
    here = lax.axis_index("dp")

    @pl.loop(0, got.shape[0])
    def _(k):
        slot = table[ids[k]]
        place = slot % own
        step = (slot // own) ^ here
        for j in range(1, dp_count):

            @pl.when(step == j)
            def _():
                sends[j - 1][place] = got[k]


def sum_kernel(dp_count, kv_rows, ids, table, got, *refs):
    received, (down, up) = refs[: dp_count - 1], refs[dp_count - 1 :]
    own, rank, rows = down.shape
    here = lax.axis_index("dp")
    tiles = rows // lanes

    @pl.loop(0, got.shape[0])
    def _(k):
        slot = table[ids[k]]
        place = slot % own

        @pl.when(slot // own == here)
        def _():
            total = got[k].astype(F32)
            for ref in received:
                total += ref[place].astype(F32)
            total = total.astype(BF16)
            for c in range(tiles):
                down[place, :, c * lanes : (c + 1) * lanes] = total[c * rank : (c + 1) * rank]
            up[place] = unpack_up(total[tiles * rank :], kv_rows, rank)


def sum_halves_kernel(dp_count, kv_rows, *refs):
    slots, got, (own_down, *sends, up, place_of) = (
        refs[:dp_count], refs[dp_count], refs[dp_count + 1 :],
    )
    own, rank, width = own_down.shape
    tiles = width // lanes
    here = lax.axis_index("dp")

    @pl.loop(0, slots[0].shape[0])
    def _(k):
        for j in range(dp_count):
            place_of[j, slots[j][k]] = k * dp_count + (here ^ j)

    for step, out in enumerate([own_down, *sends]):

        @pl.loop(0, own)
        def _(place):
            slot = (here ^ step) * own + place
            total = got[place_of[0, slot]].astype(F32)
            for j in range(1, dp_count):
                total += got[place_of[j, slot]].astype(F32)
            total = total.astype(BF16)
            for c in range(tiles):
                out[place, :, c * lanes : (c + 1) * lanes] = total[c * rank : (c + 1) * rank]
            if step == 0:
                up[place] = unpack_up(total[tiles * rank :], kv_rows, rank)


def join_kernel(dp_count, *refs):
    parts, out = refs[:-1], refs[-1]
    width = parts[0].shape[2]
    here = lax.axis_index("dp")
    for step, part in enumerate(parts):
        out[:, :, pl.ds(pl.multiple_of((here ^ step) * width, lanes), width)] = part[...]


def vmem(count):
    return [pl.BlockSpec(memory_space=pltpu.VMEM)] * count


def smem(count):
    return [pl.BlockSpec(memory_space=pltpu.SMEM)] * count


def bits(count):
    return [1 << n for n in range(count.bit_length() - 1)]


def axis_count(axis):
    names = (axis,) if isinstance(axis, str) else axis
    return math.prod(lax.axis_size(name) for name in names)


def exchange(name, array, axis, bits):
    with jax.named_scope(name):
        return lax.ppermute(array, axis, xor_pairs(axis_count(axis), bits))


def xor_pairs(count, bits):
    return [(n, n ^ bits) for n in range(count)]


def on_device(inputs, grad_value, w_value, adapter_down, adapter_up, tenant_ids, slot_table):
    tokens, width = inputs.shape
    kv_width = grad_value.shape[1]
    own, rows, rank = adapter_down.shape
    kv_rows = adapter_up.shape[1]
    fsdp_count = lax.axis_size("fsdp")
    dp_count = lax.axis_size("dp")
    inner_count = 1
    while inner_count * inner_count < fsdp_count:
        inner_count *= 2
    layers = fsdp_count // inner_count
    split = 1
    while split * 2 <= dp_count and rows // (split * 2) >= lanes:
        split *= 2
    cols = rows // split
    tall = rows // lanes * rank + packed_rows(kv_rows)[0]

    down_t = adapter_down.transpose(0, 2, 1)
    downs, ups = [down_t], [adapter_up]
    for j in range(1, dp_count):
        downs.append(exchange("down_dp", down_t, "dp", j))
        ups.append(exchange("up_dp", adapter_up, "dp", j))
    with jax.named_scope("ids"):
        ids = lax.all_to_all(
            jnp.broadcast_to(tenant_ids[:, None, None], (fsdp_count, 1, lanes)), "fsdp", 0, 0, tiled=True
        )[:, 0, 0]

    w_here = lax.dynamic_slice_in_dim(w_value, lax.axis_index("dp") % split * cols, cols, 0)
    ws = [w_here] + [None] * (layers - 1)
    for bit in bits(layers):
        ws[bit] = exchange("w_layers", w_here, "fsdp", bit * inner_count)
    gs, g_counts, rels, held = [grad_value], [1], [(0, 0)], grad_value
    stages = [("fsdp", bit) for bit in bits(inner_count)[1:]] + [("dp", bit) for bit in bits(split)]
    for n, (axis, bit) in enumerate(stages):
        new = exchange("g_" + axis, held, axis, bit)
        gs, g_counts = gs + [new], g_counts + [len(rels)]
        rels = rels + [(i | bit, d) if axis == "fsdp" else (i, d | bit) for i, d in rels]
        if n + 1 < len(stages):
            held = jnp.concatenate([held, new], axis=0)
    ids, downs, ups, gs = lax.optimization_barrier((ids, downs, ups, gs))

    box = jax.ShapeDtypeStruct((fsdp_count, tall, lanes), BF16)
    box_bytes = 2 * fsdp_count * tall * lanes
    sent = pl.pallas_call(
        functools.partial(select_kernel, dp_count),
        out_shape=box,
        in_specs=smem(2) + vmem(2 * dp_count),
        out_specs=pl.BlockSpec(memory_space=pltpu.VMEM),
        compiler_params=params(),
        cost_estimate=cost(0, 2 * box_bytes),
        name="select",
    )(ids, slot_table, *downs, *ups)
    with jax.named_scope("adapters_to_blocks"):
        got = lax.all_to_all(sent, "fsdp", 0, 0, tiled=True)
    for bit in reversed(bits(layers)):
        for k in range(0, layers, 2 * bit):
            if ws[k + bit] is None:
                ws[k + bit] = exchange("w_last", ws[k], "fsdp", bit * inner_count)
    ws = ws + [exchange("w_core", w, "fsdp", 1) for w in ws]

    pieces = pl.pallas_call(
        functools.partial(base_kernel, g_counts, len(ws)),
        out_shape=[jax.ShapeDtypeStruct((tokens, len(ws) * cols), BF16)] * len(rels),
        in_specs=vmem(len(gs) + len(ws)),
        out_specs=vmem(len(rels)),
        compiler_params=params(),
        cost_estimate=cost(
            12 * 2 * tokens * width * kv_width, 12 * 4 * tokens * width
        ),
        name="base",
    )(*gs, *ws)
    pieces = [pieces[0]] + [
        exchange("pieces%d%d" % (i, d), p, ("fsdp", "dp"), i * dp_count + d)
        for (i, d), p in zip(rels[1:], pieces[1:])
    ]
    got, pieces[:-1] = lax.optimization_barrier((got, pieces[:-1]))

    tiles = rows // lanes
    halves = dp_count if tiles % dp_count == 0 else 1
    cut = tiles // halves * rank
    small = packed_rows(kv_rows)[0]
    back_shape = (fsdp_count * halves, cut + small, lanes)
    hidden, back = pl.pallas_call(
        functools.partial(middle_kernel, kv_rows, rank, halves),
        out_shape=[
            jax.ShapeDtypeStruct((tokens, rank), BF16),
            pltpu.HBM(back_shape, BF16),
        ],
        in_specs=vmem(3),
        out_specs=vmem(1) + [pl.BlockSpec(memory_space=pltpu.HBM)],
        scratch_shapes=[
            pltpu.VMEM((fsdp_count * halves, cut, lanes), BF16),
            pltpu.VMEM((fsdp_count * halves, small, lanes), BF16),
            pltpu.SemaphoreType.DMA((store_parts + 1,)),
        ],
        compiler_params=params(),
        cost_estimate=cost(4 * tokens * width * rank, 2 * tokens * width + 2 * box_bytes),
        name="middle",
    )(inputs, grad_value, got)
    with jax.named_scope("gradients_back"):
        axes = "fsdp" if halves == 1 else ("fsdp", "dp")
        returned = lax.all_to_all(back, axes, 0, 0, tiled=True)
    if halves > 1:
        slots = jnp.sum(
            jnp.where(
                ids[:, None] == jnp.arange(slot_table.shape[0])[None, :], slot_table[None, :], 0
            ),
            axis=1,
        )
        all_slots = [slots] + [exchange("slots_dp", slots, "dp", j) for j in range(1, dp_count)]
        returned, all_slots = lax.optimization_barrier((returned, all_slots))
    returned, pieces = lax.optimization_barrier((returned, pieces))

    input_gradient_rows = pl.pallas_call(
        functools.partial(out_kernel, rels, layers, inner_count, split, rows, rank),
        out_shape=jax.ShapeDtypeStruct((tokens, width), BF16),
        in_specs=vmem(2 + len(rels)),
        out_specs=pl.BlockSpec(memory_space=pltpu.VMEM),
        compiler_params=params(),
        cost_estimate=cost(2 * tokens * width * rank, 4 * tokens * width + box_bytes),
        name="rows",
    )(hidden, got, *pieces)

    if halves > 1:
        part = (own, rank, rows // halves)
        *sums, grad_up = pl.pallas_call(
            functools.partial(sum_halves_kernel, dp_count, kv_rows),
            out_shape=[jax.ShapeDtypeStruct(part, BF16)] * dp_count
            + [jax.ShapeDtypeStruct(adapter_up.shape, BF16)],
            in_specs=smem(dp_count) + vmem(1),
            out_specs=vmem(dp_count + 1),
            scratch_shapes=[pltpu.SMEM((dp_count, own * dp_count), jnp.int32)],
            compiler_params=params(),
            cost_estimate=cost(0, 2 * box_bytes),
            name="sum_halves",
        )(*all_slots, returned)
        received = [exchange("grads_dp", s, "dp", j) for j, s in enumerate(sums[1:], 1)]
        received, input_gradient_rows = lax.optimization_barrier((received, input_gradient_rows))
        grad_down_t = pl.pallas_call(
            functools.partial(join_kernel, dp_count),
            out_shape=jax.ShapeDtypeStruct((own, rank, rows), BF16),
            in_specs=vmem(dp_count),
            out_specs=pl.BlockSpec(memory_space=pltpu.VMEM),
            compiler_params=params(),
            cost_estimate=cost(0, 4 * own * rank * rows),
            name="join",
        )(sums[0], *received)
    else:
        sends = pl.pallas_call(
            functools.partial(sort_kernel, dp_count, own),
            out_shape=[jax.ShapeDtypeStruct((own, tall, lanes), BF16)] * (dp_count - 1),
            in_specs=smem(2) + vmem(1),
            out_specs=vmem(dp_count - 1),
            compiler_params=params(),
            cost_estimate=cost(0, 2 * box_bytes),
            name="sort",
        )(ids, slot_table, returned)
        received = [
            exchange("grads_dp", s, "dp", j + 1) for j, s in enumerate(sends)
        ]
        received, input_gradient_rows = lax.optimization_barrier((received, input_gradient_rows))
        grad_down_t, grad_up = pl.pallas_call(
            functools.partial(sum_kernel, dp_count, kv_rows),
            out_shape=[
                jax.ShapeDtypeStruct((own, rank, rows), BF16),
                jax.ShapeDtypeStruct(adapter_up.shape, BF16),
            ],
            in_specs=smem(2) + vmem(dp_count),
            out_specs=vmem(2),
            compiler_params=params(),
            cost_estimate=cost(0, 2 * box_bytes),
            name="sums",
        )(ids, slot_table, returned, *received)

    return (input_gradient_rows, grad_down_t.transpose(0, 2, 1), grad_up)


def solution(mesh):
    in_specs = (
        P(("fsdp", "dp"), None),
        P(("fsdp", "dp"), None),
        P("fsdp", None),
        P("dp", "fsdp", None),
        P("dp", "fsdp", None),
        P(("fsdp", "dp")),
        P(),
    )
    out_specs = (P(("fsdp", "dp"), None), P("dp", "fsdp", None), P("dp", "fsdp", None))
    return jax.shard_map(
        on_device, mesh=mesh, in_specs=in_specs, out_specs=out_specs, check_vma=False
    )
```

```python
import functools
import math

import jax
import jax.numpy as jnp
from jax import lax
from jax.experimental import pallas as pl
from jax.experimental.pallas import tpu as pltpu
from jax.sharding import PartitionSpec as P

adapter_scale_factor = 2.0
lanes = 128
base_weight = 11
store_parts = 4
BF16, F32 = jnp.bfloat16, jnp.float32
NT = (((1,), (1,)), ((), ()))
TN = (((0,), (0,)), ((), ()))
NN = (((1,), (0,)), ((), ()))


def params():
    return pltpu.CompilerParams(vmem_limit_bytes=40 * 1024 * 1024)


def cost(flops, nbytes):
    return pl.CostEstimate(flops=flops, bytes_accessed=nbytes, transcendentals=0)


def dot(a, b, dims):
    return lax.dot_general(a, b, dims, preferred_element_type=F32)


def packed_rows(kv_rows):
    if kv_rows % 32 == 0:
        return kv_rows // 2, 2
    return -(-kv_rows // 16) * 16, 1


def pack_up(block):
    kv_rows, rank = block.shape
    rows, groups = packed_rows(kv_rows)
    if groups == 2:
        return jnp.concatenate([block[:rows], block[rows:]], axis=1)
    block = jnp.concatenate([block, jnp.zeros((kv_rows, lanes - rank), block.dtype)], axis=1)
    if rows == kv_rows:
        return block
    return jnp.concatenate([block, jnp.zeros((rows - kv_rows, lanes), block.dtype)], axis=0)


def unpack_up(packed, kv_rows, rank):
    rows, groups = packed_rows(kv_rows)
    if groups == 2:
        return jnp.concatenate([packed[:, :rank], packed[:, rank:]], axis=0)
    return packed[:kv_rows, :rank]


def wide(ref, index, first, count, rank):
    return jnp.concatenate(
        [
            ref[index, pl.ds(pl.multiple_of((first + j) * rank, 16), rank), :]
            for j in range(count)
        ],
        axis=1,
    )


def select_kernel(dp_count, slots, *refs):
    downs, ups, (out, held, sems) = (
        refs[:dp_count], refs[dp_count : 2 * dp_count], refs[2 * dp_count :],
    )
    own, rank, rows = downs[0].shape
    here = lax.axis_index("dp")
    cut = rows // lanes * rank

    @pl.loop(0, out.shape[0])
    def _(k):
        place = slots[k] % own
        step = (slots[k] // own) ^ here
        for j in range(dp_count):

            @pl.when(step == j)
            def _():
                for c in range(rows // lanes):
                    held[k, c * rank : (c + 1) * rank, :] = downs[j][
                        place, :, c * lanes : (c + 1) * lanes
                    ]
                held[k, cut:, :] = pack_up(ups[j][place])

        pltpu.make_async_copy(held.at[k], out.at[k], sems.at[k]).start()

    @pl.loop(0, out.shape[0])
    def _(k):
        pltpu.make_async_copy(held.at[k], out.at[k], sems.at[k]).wait()


def middle_kernel(kv_rows, rank, halves, x, g, got, hidden_out, back, out, up_out, sems):
    fsdp_count = got.shape[0]
    tiles = x.shape[1] // fsdp_count // lanes
    rows = tiles * lanes
    cut = tiles * rank
    up = jnp.concatenate(
        [unpack_up(got[f, cut:, :], kv_rows, rank) for f in range(fsdp_count)], axis=0
    )
    hidden = dot(g[...], up, NN).astype(BF16)
    hidden_out[...] = hidden
    inner = jnp.zeros((x.shape[0], rank), F32)
    stores = []
    step = max(1, fsdp_count // store_parts)
    for f in range(fsdp_count):
        x_part = x[:, f * rows : (f + 1) * rows]
        inner += dot(x_part, wide(got, f, 0, tiles, rank), NT)
        down = (adapter_scale_factor * dot(hidden, x_part, TN)).astype(BF16)
        for c in range(tiles):
            half, at = c * halves // tiles, c % (tiles // halves) * rank
            out[f * halves + half, at : at + rank, :] = down[:, c * lanes : (c + 1) * lanes]
        if (f + 1) % step == 0:
            here = pl.ds((f + 1 - step) * halves, step * halves)
            stores.append(
                pltpu.make_async_copy(
                    out.at[here], back.at[here, 0 : out.shape[1], :], sems.at[len(stores)]
                )
            )
            stores[-1].start()
    part_up = (adapter_scale_factor * dot(g[...], inner.astype(BF16), TN)).astype(BF16)
    for f in range(fsdp_count):
        packed = pack_up(part_up[f * kv_rows : (f + 1) * kv_rows])
        for half in range(halves):
            up_out[f * halves + half] = packed
    stores.append(
        pltpu.make_async_copy(
            up_out,
            back.at[:, out.shape[1] : out.shape[1] + up_out.shape[1], :],
            sems.at[len(stores)],
        )
    )
    stores[-1].start()
    for store in stores:
        store.wait()


def base_kernel(g_counts, w_count, *refs):
    gs, ws = refs[: len(g_counts)], refs[len(g_counts) : len(g_counts) + w_count]
    outs = refs[len(g_counts) + w_count :]
    at = 0
    cols = ws[0].shape[0]
    for ref, count in zip(gs, g_counts):
        rows = ref.shape[0] // count
        for n in range(count):
            for k in range(w_count):
                outs[at][:, k * cols : (k + 1) * cols] = dot(
                    ref[n * rows : (n + 1) * rows, :], ws[k][...], NT
                ).astype(BF16)
            at += 1


def out_kernel(rels, layers, inner_count, split, rows, rank, hidden, got, *refs):
    pieces, out = refs[:-1], refs[-1]
    f_here = lax.axis_index("fsdp")
    d_here = lax.axis_index("dp") % split
    cols = rows // split
    tiles = cols // lanes
    h = hidden[...]
    for (i_rel, d_rel), piece in zip(rels, pieces):
        d = d_here ^ d_rel
        for k in range(2 * layers):
            f = f_here ^ (k % layers * inner_count + k // layers + i_rel)
            adapter = wide(got, f, d * tiles, tiles, rank)
            low = adapter_scale_factor * dot(h, adapter, NN)
            start = pl.multiple_of(f * rows + d * cols, lanes)
            out[:, pl.ds(start, cols)] = (
                piece[:, k * cols : (k + 1) * cols].astype(F32) + low
            ).astype(BF16)


def sort_kernel(dp_count, own, slots, got, *sends):
    here = lax.axis_index("dp")

    @pl.loop(0, got.shape[0])
    def _(k):
        slot = slots[k]
        place = slot % own
        step = (slot // own) ^ here
        for j in range(1, dp_count):

            @pl.when(step == j)
            def _():
                sends[j - 1][place] = got[k]


def sum_kernel(dp_count, kv_rows, slots, got, *refs):
    received, (down, up) = refs[: dp_count - 1], refs[dp_count - 1 :]
    own, rank, rows = down.shape
    here = lax.axis_index("dp")
    tiles = rows // lanes

    @pl.loop(0, got.shape[0])
    def _(k):
        slot = slots[k]
        place = slot % own

        @pl.when(slot // own == here)
        def _():
            total = got[k].astype(F32)
            for ref in received:
                total += ref[place].astype(F32)
            total = total.astype(BF16)
            for c in range(tiles):
                down[place, :, c * lanes : (c + 1) * lanes] = total[c * rank : (c + 1) * rank]
            up[place] = unpack_up(total[tiles * rank :], kv_rows, rank)


def sum_halves_kernel(dp_count, kv_rows, first, steps, *refs):
    slots, got, outs, place_of = refs[:dp_count], refs[dp_count], refs[dp_count + 1 : -1], refs[-1]
    own, rank, width = outs[0].shape
    tiles = width // lanes
    here = lax.axis_index("dp")

    @pl.loop(0, slots[0].shape[0])
    def _(k):
        for j in range(dp_count):
            place_of[j, slots[j][k]] = k * dp_count + (here ^ j)

    for step, out in zip(range(first, first + steps), outs):

        @pl.loop(0, own)
        def _(place):
            slot = (here ^ step) * own + place
            total = got[place_of[0, slot]].astype(F32)
            for j in range(1, dp_count):
                total += got[place_of[j, slot]].astype(F32)
            total = total.astype(BF16)
            for c in range(tiles):
                out[place, :, c * lanes : (c + 1) * lanes] = total[c * rank : (c + 1) * rank]
            if step == 0:
                outs[-1][place] = unpack_up(total[tiles * rank :], kv_rows, rank)


def join_kernel(dp_count, *refs):
    parts, out = refs[:-1], refs[-1]
    width = parts[0].shape[2]
    here = lax.axis_index("dp")
    for step, part in enumerate(parts):
        out[:, :, pl.ds(pl.multiple_of((here ^ step) * width, lanes), width)] = part[...]


def vmem(count):
    return [pl.BlockSpec(memory_space=pltpu.VMEM)] * count


def smem(count):
    return [pl.BlockSpec(memory_space=pltpu.SMEM)] * count


def bits(count):
    return [1 << n for n in range(count.bit_length() - 1)]


def axis_count(axis):
    names = (axis,) if isinstance(axis, str) else axis
    return math.prod(lax.axis_size(name) for name in names)


def exchange(name, array, axis, bits):
    with jax.named_scope(name):
        return lax.ppermute(array, axis, xor_pairs(axis_count(axis), bits))


def xor_pairs(count, bits):
    return [(n, n ^ bits) for n in range(count)]


def on_device(inputs, grad_value, w_value, adapter_down, adapter_up, tenant_ids, slot_table):
    tokens, width = inputs.shape
    kv_width = grad_value.shape[1]
    own, rows, rank = adapter_down.shape
    kv_rows = adapter_up.shape[1]
    fsdp_count = lax.axis_size("fsdp")
    dp_count = lax.axis_size("dp")
    inner_count = 1
    while inner_count * inner_count < fsdp_count:
        inner_count *= 2
    layers = fsdp_count // inner_count
    split = 1
    while split * 2 <= dp_count and rows // (split * 2) >= lanes:
        split *= 2
    cols = rows // split
    tall = rows // lanes * rank + packed_rows(kv_rows)[0]

    down_t = adapter_down.transpose(0, 2, 1)
    downs, ups = [down_t], [adapter_up]
    for j in range(1, dp_count):
        downs.append(exchange("down_dp", down_t, "dp", j))
        ups.append(exchange("up_dp", adapter_up, "dp", j))
    with jax.named_scope("ids"):
        ids = lax.all_to_all(
            jnp.broadcast_to(tenant_ids[:, None, None], (fsdp_count, 1, lanes)), "fsdp", 0, 0, tiled=True
        )[:, 0, 0]

    w_here = lax.dynamic_slice_in_dim(w_value, lax.axis_index("dp") % split * cols, cols, 0)
    ws = [w_here] + [None] * (layers - 1)
    for bit in bits(layers):
        ws[bit] = exchange("w_layers", w_here, "fsdp", bit * inner_count)
    gs, rels = [grad_value], [(0, 0)]
    stages = [("fsdp", bit) for bit in bits(inner_count)[1:]] + [("dp", bit) for bit in bits(split)]
    for axis, bit in stages:
        gs = gs + [exchange("g_" + axis, g, axis, bit) for g in gs]
        rels = rels + [(i | bit, d) if axis == "fsdp" else (i, d | bit) for i, d in rels]
    g_counts = [1] * len(rels)
    ids, downs, ups, ws, gs[1] = lax.optimization_barrier((ids, downs, ups, ws, gs[1]))

    box = jax.ShapeDtypeStruct((fsdp_count, tall, lanes), BF16)
    box_bytes = 2 * fsdp_count * tall * lanes
    slots = jnp.sum(
        jnp.where(
            ids[:, None] == jnp.arange(slot_table.shape[0])[None, :], slot_table[None, :], 0
        ),
        axis=1,
    )
    ups[0] = pltpu.with_memory_space_constraint(ups[0], pltpu.HBM)
    sent = pl.pallas_call(
        functools.partial(select_kernel, dp_count),
        out_shape=pltpu.HBM(box.shape, BF16),
        in_specs=smem(1) + vmem(2 * dp_count),
        out_specs=pl.BlockSpec(memory_space=pltpu.HBM),
        scratch_shapes=[
            pltpu.VMEM(box.shape, BF16), pltpu.SemaphoreType.DMA((fsdp_count,)),
        ],
        compiler_params=params(),
        cost_estimate=cost(0, 2 * box_bytes),
        name="select",
    )(slots, *downs, *ups)
    with jax.named_scope("adapters_to_blocks"):
        got = lax.all_to_all(sent, "fsdp", 0, 0, tiled=True)
    for bit in reversed(bits(layers)):
        for k in range(0, layers, 2 * bit):
            if ws[k + bit] is None:
                ws[k + bit] = exchange("w_last", ws[k], "fsdp", bit * inner_count)
    ws = ws + [exchange("w_core", w, "fsdp", 1) for w in ws]

    pieces = pl.pallas_call(
        functools.partial(base_kernel, g_counts, len(ws)),
        out_shape=[jax.ShapeDtypeStruct((tokens, len(ws) * cols), BF16)] * len(rels),
        in_specs=vmem(len(gs) + len(ws)),
        out_specs=vmem(len(rels)),
        compiler_params=params(),
        cost_estimate=cost(
            base_weight * 2 * tokens * width * kv_width, base_weight * 4 * tokens * width
        ),
        name="base",
    )(*gs, *ws)
    pieces = [pieces[0]] + [
        exchange("pieces%d%d" % (i, d), p, ("fsdp", "dp"), i * dp_count + d)
        for (i, d), p in zip(rels[1:], pieces[1:])
    ]
    got, pieces[:-1] = lax.optimization_barrier((got, pieces[:-1]))

    tiles = rows // lanes
    halves = dp_count if tiles % dp_count == 0 else 1
    cut = tiles // halves * rank
    small = packed_rows(kv_rows)[0]
    back_shape = (fsdp_count * halves, cut + small, lanes)
    hidden, back = pl.pallas_call(
        functools.partial(middle_kernel, kv_rows, rank, halves),
        out_shape=[
            jax.ShapeDtypeStruct((tokens, rank), BF16),
            pltpu.HBM(back_shape, BF16),
        ],
        in_specs=vmem(3),
        out_specs=vmem(1) + [pl.BlockSpec(memory_space=pltpu.HBM)],
        scratch_shapes=[
            pltpu.VMEM((fsdp_count * halves, cut, lanes), BF16),
            pltpu.VMEM((fsdp_count * halves, small, lanes), BF16),
            pltpu.SemaphoreType.DMA((store_parts + 1,)),
        ],
        compiler_params=params(),
        cost_estimate=cost(4 * tokens * width * rank, 2 * tokens * width + 2 * box_bytes),
        name="middle",
    )(inputs, grad_value, got)
    with jax.named_scope("gradients_back"):
        axes = "fsdp" if halves == 1 else ("fsdp", "dp")
        returned = lax.all_to_all(back, axes, 0, 0, tiled=True)
    if halves > 1:
        all_slots = [slots] + [exchange("slots_dp", slots, "dp", j) for j in range(1, dp_count)]
        returned, all_slots = lax.optimization_barrier((returned, all_slots))
    returned, pieces = lax.optimization_barrier((returned, pieces))

    input_gradient_rows = pl.pallas_call(
        functools.partial(out_kernel, rels, layers, inner_count, split, rows, rank),
        out_shape=jax.ShapeDtypeStruct((tokens, width), BF16),
        in_specs=vmem(2 + len(rels)),
        out_specs=pl.BlockSpec(memory_space=pltpu.VMEM),
        compiler_params=params(),
        cost_estimate=cost(2 * tokens * width * rank, 4 * tokens * width + box_bytes),
        name="rows",
    )(hidden, got, *pieces)

    if halves > 1:
        part = (own, rank, rows // halves)

        def sum_halves(first, steps, extra, name):
            return pl.pallas_call(
                functools.partial(sum_halves_kernel, dp_count, kv_rows, first, steps),
                out_shape=[jax.ShapeDtypeStruct(shape, BF16) for shape in [part] * steps + extra],
                in_specs=smem(dp_count) + vmem(1),
                out_specs=vmem(steps + len(extra)),
                scratch_shapes=[pltpu.SMEM((dp_count, own * dp_count), jnp.int32)],
                compiler_params=params(),
                cost_estimate=cost(0, 2 * box_bytes),
                name=name,
            )(*all_slots, returned)

        *sums, grad_up = sum_halves(0, dp_count, [adapter_up.shape], "sum_all")
        received = [exchange("grads_dp", s, "dp", j) for j, s in enumerate(sums[1:], 1)]
        received, input_gradient_rows, sums[0], grad_up = lax.optimization_barrier(
            (received, input_gradient_rows, sums[0], grad_up)
        )
        grad_down_t = pl.pallas_call(
            functools.partial(join_kernel, dp_count),
            out_shape=jax.ShapeDtypeStruct((own, rank, rows), BF16),
            in_specs=vmem(dp_count),
            out_specs=pl.BlockSpec(memory_space=pltpu.VMEM),
            compiler_params=params(),
            cost_estimate=cost(0, 4 * own * rank * rows),
            name="join",
        )(sums[0], *received)
    else:
        sends = pl.pallas_call(
            functools.partial(sort_kernel, dp_count, own),
            out_shape=[jax.ShapeDtypeStruct((own, tall, lanes), BF16)] * (dp_count - 1),
            in_specs=smem(1) + vmem(1),
            out_specs=vmem(dp_count - 1),
            compiler_params=params(),
            cost_estimate=cost(0, 2 * box_bytes),
            name="sort",
        )(slots, returned)
        received = [
            exchange("grads_dp", s, "dp", j + 1) for j, s in enumerate(sends)
        ]
        received, input_gradient_rows = lax.optimization_barrier((received, input_gradient_rows))
        grad_down_t, grad_up = pl.pallas_call(
            functools.partial(sum_kernel, dp_count, kv_rows),
            out_shape=[
                jax.ShapeDtypeStruct((own, rank, rows), BF16),
                jax.ShapeDtypeStruct(adapter_up.shape, BF16),
            ],
            in_specs=smem(1) + vmem(dp_count),
            out_specs=vmem(2),
            compiler_params=params(),
            cost_estimate=cost(0, 2 * box_bytes),
            name="sums",
        )(slots, returned, *received)

    return (input_gradient_rows, grad_down_t.transpose(0, 2, 1), grad_up)


def solution(mesh):
    in_specs = (
        P(("fsdp", "dp"), None),
        P(("fsdp", "dp"), None),
        P("fsdp", None),
        P("dp", "fsdp", None),
        P("dp", "fsdp", None),
        P(("fsdp", "dp")),
        P(),
    )
    out_specs = (P(("fsdp", "dp"), None), P("dp", "fsdp", None), P("dp", "fsdp", None))
    return jax.shard_map(
        on_device, mesh=mesh, in_specs=in_specs, out_specs=out_specs, check_vma=False
    )
```

```python
import functools
import math

import jax
import jax.numpy as jnp
from jax import lax
from jax.experimental import pallas as pl
from jax.experimental.pallas import tpu as pltpu
from jax.sharding import PartitionSpec as P

adapter_scale_factor = 2.0
lanes = 128
base_weight = 11
store_parts = 4
BF16, F32 = jnp.bfloat16, jnp.float32
NT = (((1,), (1,)), ((), ()))
TN = (((0,), (0,)), ((), ()))
NN = (((1,), (0,)), ((), ()))


def params():
    return pltpu.CompilerParams(vmem_limit_bytes=40 * 1024 * 1024)


def cost(flops, nbytes):
    return pl.CostEstimate(flops=flops, bytes_accessed=nbytes, transcendentals=0)


def dot(a, b, dims):
    return lax.dot_general(a, b, dims, preferred_element_type=F32)


def packed_rows(kv_rows):
    if kv_rows % 32 == 0:
        return kv_rows // 2, 2
    return -(-kv_rows // 16) * 16, 1


def pack_up(block):
    kv_rows, rank = block.shape
    rows, groups = packed_rows(kv_rows)
    if groups == 2:
        return jnp.concatenate([block[:rows], block[rows:]], axis=1)
    block = jnp.concatenate([block, jnp.zeros((kv_rows, lanes - rank), block.dtype)], axis=1)
    if rows == kv_rows:
        return block
    return jnp.concatenate([block, jnp.zeros((rows - kv_rows, lanes), block.dtype)], axis=0)


def unpack_up(packed, kv_rows, rank):
    rows, groups = packed_rows(kv_rows)
    if groups == 2:
        return jnp.concatenate([packed[:, :rank], packed[:, rank:]], axis=0)
    return packed[:kv_rows, :rank]


def wide(ref, index, first, count, rank):
    return jnp.concatenate(
        [
            ref[index, pl.ds(pl.multiple_of((first + j) * rank, 16), rank), :]
            for j in range(count)
        ],
        axis=1,
    )


def select_kernel(dp_count, slots, *refs):
    downs, ups, (out, held, sems) = (
        refs[:dp_count], refs[dp_count : 2 * dp_count], refs[2 * dp_count :],
    )
    own, rank, rows = downs[0].shape
    here = lax.axis_index("dp")
    cut = rows // lanes * rank

    @pl.loop(0, out.shape[0])
    def _(k):
        place = slots[k] % own
        step = (slots[k] // own) ^ here
        for j in range(dp_count):

            @pl.when(step == j)
            def _():
                for c in range(rows // lanes):
                    held[k, c * rank : (c + 1) * rank, :] = downs[j][
                        place, :, c * lanes : (c + 1) * lanes
                    ]
                held[k, cut:, :] = pack_up(ups[j][place])

        pltpu.make_async_copy(held.at[k], out.at[k], sems.at[k]).start()

    @pl.loop(0, out.shape[0])
    def _(k):
        pltpu.make_async_copy(held.at[k], out.at[k], sems.at[k]).wait()


def middle_kernel(kv_rows, rank, halves, x, g, got, hidden_out, back, out, up_out, sems):
    fsdp_count = got.shape[0]
    tiles = x.shape[1] // fsdp_count // lanes
    rows = tiles * lanes
    cut = tiles * rank
    up = jnp.concatenate(
        [unpack_up(got[f, cut:, :], kv_rows, rank) for f in range(fsdp_count)], axis=0
    )
    hidden = dot(g[...], up, NN).astype(BF16)
    hidden_out[...] = hidden
    inner = jnp.zeros((x.shape[0], rank), F32)
    stores = []
    step = max(1, fsdp_count // store_parts)
    for f in range(fsdp_count):
        x_part = x[:, f * rows : (f + 1) * rows]
        inner += dot(x_part, wide(got, f, 0, tiles, rank), NT)
        down = (adapter_scale_factor * dot(hidden, x_part, TN)).astype(BF16)
        for c in range(tiles):
            half, at = c * halves // tiles, c % (tiles // halves) * rank
            out[f * halves + half, at : at + rank, :] = down[:, c * lanes : (c + 1) * lanes]
        if (f + 1) % step == 0:
            here = pl.ds((f + 1 - step) * halves, step * halves)
            stores.append(
                pltpu.make_async_copy(
                    out.at[here], back.at[here, 0 : out.shape[1], :], sems.at[len(stores)]
                )
            )
            stores[-1].start()
    part_up = (adapter_scale_factor * dot(g[...], inner.astype(BF16), TN)).astype(BF16)
    for f in range(fsdp_count):
        packed = pack_up(part_up[f * kv_rows : (f + 1) * kv_rows])
        for half in range(halves):
            up_out[f * halves + half] = packed
    stores.append(
        pltpu.make_async_copy(
            up_out,
            back.at[:, out.shape[1] : out.shape[1] + up_out.shape[1], :],
            sems.at[len(stores)],
        )
    )
    stores[-1].start()
    for store in stores:
        store.wait()


def base_kernel(rels, near_count, layers, own, *refs):
    near, refs = refs[:near_count], refs[near_count:]
    outs, refs = refs[-len(rels) :], refs[: -len(rels)]
    ws, near_other, others = (
        refs[: 2 * layers],
        refs[2 * layers : 2 * layers + near_count],
        refs[2 * layers + near_count :],
    )
    tokens = own.shape[0]
    cols = ws[0].shape[0]
    here = [w[...] for w in ws]
    beside = [ref[tokens:, :] for pair in zip(near, near_other) for ref in pair]
    gs = [own[...]] + [ref[:tokens, :] for ref in near]
    gs += [
        ref[n * tokens : (n + 1) * tokens, :] for ref in others for n in range(near_count + 1)
    ]
    for (i, _), g, out in zip(rels, gs, outs):
        if i == 0:
            parts = here + beside
        else:
            parts = here[1:layers] + here[layers + 1 :]
        for k, w in enumerate(parts):
            out[:, k * cols : (k + 1) * cols] = dot(g, w, NT).astype(BF16)


def out_kernel(rels, layers, inner_count, split, rows, rank, hidden, got, *refs):
    pieces, out = refs[:-1], refs[-1]
    f_here = lax.axis_index("fsdp")
    d_here = lax.axis_index("dp") % split
    cols = rows // split
    tiles = cols // lanes
    h = hidden[...]
    far = [k * inner_count + core for core in range(2) for k in range(1, layers)]
    every = [k * inner_count + core for core in range(2) for k in range(layers)]
    every += [i + core for i in range(2, inner_count, 2) for core in range(2)]
    for (i_rel, d_rel), piece in zip(rels, pieces):
        d = d_here ^ d_rel
        for k, f_rel in enumerate(every if i_rel == 0 else far):
            f = f_here ^ (f_rel ^ i_rel)
            low = adapter_scale_factor * dot(h, wide(got, f, d * tiles, tiles, rank), NN)
            start = pl.multiple_of(f * rows + d * cols, lanes)
            out[:, pl.ds(start, cols)] = (
                piece[:, k * cols : (k + 1) * cols].astype(F32) + low
            ).astype(BF16)


def sort_kernel(dp_count, own, slots, got, *sends):
    here = lax.axis_index("dp")

    @pl.loop(0, got.shape[0])
    def _(k):
        slot = slots[k]
        place = slot % own
        step = (slot // own) ^ here
        for j in range(1, dp_count):

            @pl.when(step == j)
            def _():
                sends[j - 1][place] = got[k]


def sum_kernel(dp_count, kv_rows, slots, got, *refs):
    received, (down, up) = refs[: dp_count - 1], refs[dp_count - 1 :]
    own, rank, rows = down.shape
    here = lax.axis_index("dp")
    tiles = rows // lanes

    @pl.loop(0, got.shape[0])
    def _(k):
        slot = slots[k]
        place = slot % own

        @pl.when(slot // own == here)
        def _():
            total = got[k].astype(F32)
            for ref in received:
                total += ref[place].astype(F32)
            total = total.astype(BF16)
            for c in range(tiles):
                down[place, :, c * lanes : (c + 1) * lanes] = total[c * rank : (c + 1) * rank]
            up[place] = unpack_up(total[tiles * rank :], kv_rows, rank)


def sum_halves_kernel(dp_count, kv_rows, first, steps, *refs):
    slots, got, outs, place_of = refs[:dp_count], refs[dp_count], refs[dp_count + 1 : -1], refs[-1]
    own, rank, width = outs[0].shape
    tiles = width // lanes
    here = lax.axis_index("dp")

    @pl.loop(0, slots[0].shape[0])
    def _(k):
        for j in range(dp_count):
            place_of[j, slots[j][k]] = k * dp_count + (here ^ j)

    for step, out in zip(range(first, first + steps), outs):

        @pl.loop(0, own)
        def _(place):
            slot = (here ^ step) * own + place
            total = got[place_of[0, slot]].astype(F32)
            for j in range(1, dp_count):
                total += got[place_of[j, slot]].astype(F32)
            total = total.astype(BF16)
            for c in range(tiles):
                out[place, :, c * lanes : (c + 1) * lanes] = total[c * rank : (c + 1) * rank]
            if step == 0:
                outs[-1][place] = unpack_up(total[tiles * rank :], kv_rows, rank)


def join_kernel(dp_count, *refs):
    parts, out = refs[:-1], refs[-1]
    width = parts[0].shape[2]
    here = lax.axis_index("dp")
    for step, part in enumerate(parts):
        out[:, :, pl.ds(pl.multiple_of((here ^ step) * width, lanes), width)] = part[...]


def vmem(count):
    return [pl.BlockSpec(memory_space=pltpu.VMEM)] * count


def smem(count):
    return [pl.BlockSpec(memory_space=pltpu.SMEM)] * count


def bits(count):
    return [1 << n for n in range(count.bit_length() - 1)]


def axis_count(axis):
    names = (axis,) if isinstance(axis, str) else axis
    return math.prod(lax.axis_size(name) for name in names)


def exchange(name, array, axis, bits):
    with jax.named_scope(name):
        return lax.ppermute(array, axis, xor_pairs(axis_count(axis), bits))


def xor_pairs(count, bits):
    return [(n, n ^ bits) for n in range(count)]


def on_device(inputs, grad_value, w_value, adapter_down, adapter_up, tenant_ids, slot_table):
    tokens, width = inputs.shape
    kv_width = grad_value.shape[1]
    own, rows, rank = adapter_down.shape
    kv_rows = adapter_up.shape[1]
    fsdp_count = lax.axis_size("fsdp")
    dp_count = lax.axis_size("dp")
    inner_count = 1
    while inner_count * inner_count < fsdp_count:
        inner_count *= 2
    layers = fsdp_count // inner_count
    split = 1
    while split * 2 <= dp_count and rows // (split * 2) >= lanes:
        split *= 2
    cols = rows // split
    tall = rows // lanes * rank + packed_rows(kv_rows)[0]

    down_t = adapter_down.transpose(0, 2, 1)
    downs, ups = [down_t], [adapter_up]
    for j in range(1, dp_count):
        downs.append(exchange("down_dp", down_t, "dp", j))
        ups.append(exchange("up_dp", adapter_up, "dp", j))
    with jax.named_scope("ids"):
        ids = lax.all_to_all(
            jnp.broadcast_to(tenant_ids[:, None, None], (fsdp_count, 1, lanes)), "fsdp", 0, 0, tiled=True
        )[:, 0, 0]

    w_here = lax.dynamic_slice_in_dim(w_value, lax.axis_index("dp") % split * cols, cols, 0)
    ws = [w_here] + [None] * (layers - 1)
    for bit in bits(layers):
        ws[bit] = exchange("w_layers", w_here, "fsdp", bit * inner_count)
    rels = [(i, 0) for i in range(0, inner_count, 2)]
    beside = jnp.concatenate([grad_value, w_here], axis=0)
    near = [exchange("g_w_layer", beside, "fsdp", i) for i, _ in rels[1:]]
    ids, downs, ups, ws, near = lax.optimization_barrier((ids, downs, ups, ws, near))
    held = jnp.concatenate([grad_value] + [n[:tokens] for n in near], axis=0)
    others = [exchange("g_dp", held, "dp", d) for d in range(1, split)]
    rels = rels + [(i, d) for d in range(1, split) for i, _ in rels]

    box = jax.ShapeDtypeStruct((fsdp_count, tall, lanes), BF16)
    box_bytes = 2 * fsdp_count * tall * lanes
    slots = jnp.sum(
        jnp.where(
            ids[:, None] == jnp.arange(slot_table.shape[0])[None, :], slot_table[None, :], 0
        ),
        axis=1,
    )
    ups[0] = pltpu.with_memory_space_constraint(ups[0], pltpu.HBM)
    downs[0] = pltpu.with_memory_space_constraint(downs[0], pltpu.HBM)
    sent = pl.pallas_call(
        functools.partial(select_kernel, dp_count),
        out_shape=pltpu.HBM(box.shape, BF16),
        in_specs=smem(1) + vmem(2 * dp_count),
        out_specs=pl.BlockSpec(memory_space=pltpu.HBM),
        scratch_shapes=[
            pltpu.VMEM(box.shape, BF16), pltpu.SemaphoreType.DMA((fsdp_count,)),
        ],
        compiler_params=params(),
        cost_estimate=cost(0, 2 * box_bytes),
        name="select",
    )(slots, *downs, *ups)
    with jax.named_scope("adapters_to_blocks"):
        got = lax.all_to_all(sent, "fsdp", 0, 0, tiled=True)
    for bit in reversed(bits(layers)):
        for k in range(0, layers, 2 * bit):
            if ws[k + bit] is None:
                ws[k + bit] = exchange("w_last", ws[k], "fsdp", bit * inner_count)
    ws = ws + [exchange("w_core", w, "fsdp", 1) for w in ws]
    near_other = [exchange("w_core", n, "fsdp", 1) for n in near]

    wide_cols = (2 * layers + 2 * len(near)) * cols
    pieces = pl.pallas_call(
        functools.partial(base_kernel, rels, len(near), layers),
        out_shape=[
            jax.ShapeDtypeStruct((tokens, wide_cols if i == 0 else (2 * layers - 2) * cols), BF16)
            for i, _ in rels
        ],
        in_specs=vmem(1 + 2 * len(near) + len(ws) + len(others)),
        out_specs=vmem(len(rels)),
        compiler_params=params(),
        cost_estimate=cost(
            base_weight * 2 * tokens * width * kv_width, base_weight * 4 * tokens * width
        ),
        name="base",
    )(grad_value, *near, *ws, *near_other, *others)
    pieces = [pieces[0]] + [
        exchange("pieces%d%d" % (i, d), p, ("fsdp", "dp"), i * dp_count + d)
        for (i, d), p in zip(rels[1:], pieces[1:])
    ]
    got, pieces[:-1] = lax.optimization_barrier((got, pieces[:-1]))

    tiles = rows // lanes
    halves = dp_count if tiles % dp_count == 0 else 1
    cut = tiles // halves * rank
    small = packed_rows(kv_rows)[0]
    back_shape = (fsdp_count * halves, cut + small, lanes)
    hidden, back = pl.pallas_call(
        functools.partial(middle_kernel, kv_rows, rank, halves),
        out_shape=[
            jax.ShapeDtypeStruct((tokens, rank), BF16),
            pltpu.HBM(back_shape, BF16),
        ],
        in_specs=vmem(3),
        out_specs=vmem(1) + [pl.BlockSpec(memory_space=pltpu.HBM)],
        scratch_shapes=[
            pltpu.VMEM((fsdp_count * halves, cut, lanes), BF16),
            pltpu.VMEM((fsdp_count * halves, small, lanes), BF16),
            pltpu.SemaphoreType.DMA((store_parts + 1,)),
        ],
        compiler_params=params(),
        cost_estimate=cost(4 * tokens * width * rank, 2 * tokens * width + 2 * box_bytes),
        name="middle",
    )(inputs, grad_value, got)
    with jax.named_scope("gradients_back"):
        axes = "fsdp" if halves == 1 else ("fsdp", "dp")
        returned = lax.all_to_all(back, axes, 0, 0, tiled=True)
    if halves > 1:
        all_slots = [slots] + [exchange("slots_dp", slots, "dp", j) for j in range(1, dp_count)]
        returned, all_slots = lax.optimization_barrier((returned, all_slots))
    returned, pieces = lax.optimization_barrier((returned, pieces))

    input_gradient_rows = pl.pallas_call(
        functools.partial(out_kernel, rels, layers, inner_count, split, rows, rank),
        out_shape=jax.ShapeDtypeStruct((tokens, width), BF16),
        in_specs=vmem(2 + len(rels)),
        out_specs=pl.BlockSpec(memory_space=pltpu.VMEM),
        compiler_params=params(),
        cost_estimate=cost(2 * tokens * width * rank, 4 * tokens * width + box_bytes),
        name="rows",
    )(hidden, got, *pieces)

    if halves > 1:
        part = (own, rank, rows // halves)

        def sum_halves(first, steps, extra, name):
            return pl.pallas_call(
                functools.partial(sum_halves_kernel, dp_count, kv_rows, first, steps),
                out_shape=[jax.ShapeDtypeStruct(shape, BF16) for shape in [part] * steps + extra],
                in_specs=smem(dp_count) + vmem(1),
                out_specs=vmem(steps + len(extra)),
                scratch_shapes=[pltpu.SMEM((dp_count, own * dp_count), jnp.int32)],
                compiler_params=params(),
                cost_estimate=cost(0, 2 * box_bytes),
                name=name,
            )(*all_slots, returned)

        *sums, grad_up = sum_halves(0, dp_count, [adapter_up.shape], "sum_all")
        received = [exchange("grads_dp", s, "dp", j) for j, s in enumerate(sums[1:], 1)]
        received, input_gradient_rows, sums[0], grad_up = lax.optimization_barrier(
            (received, input_gradient_rows, sums[0], grad_up)
        )
        grad_down_t = pl.pallas_call(
            functools.partial(join_kernel, dp_count),
            out_shape=jax.ShapeDtypeStruct((own, rank, rows), BF16),
            in_specs=vmem(dp_count),
            out_specs=pl.BlockSpec(memory_space=pltpu.VMEM),
            compiler_params=params(),
            cost_estimate=cost(0, 4 * own * rank * rows),
            name="join",
        )(sums[0], *received)
    else:
        sends = pl.pallas_call(
            functools.partial(sort_kernel, dp_count, own),
            out_shape=[jax.ShapeDtypeStruct((own, tall, lanes), BF16)] * (dp_count - 1),
            in_specs=smem(1) + vmem(1),
            out_specs=vmem(dp_count - 1),
            compiler_params=params(),
            cost_estimate=cost(0, 2 * box_bytes),
            name="sort",
        )(slots, returned)
        received = [
            exchange("grads_dp", s, "dp", j + 1) for j, s in enumerate(sends)
        ]
        received, input_gradient_rows = lax.optimization_barrier((received, input_gradient_rows))
        grad_down_t, grad_up = pl.pallas_call(
            functools.partial(sum_kernel, dp_count, kv_rows),
            out_shape=[
                jax.ShapeDtypeStruct((own, rank, rows), BF16),
                jax.ShapeDtypeStruct(adapter_up.shape, BF16),
            ],
            in_specs=smem(1) + vmem(dp_count),
            out_specs=vmem(2),
            compiler_params=params(),
            cost_estimate=cost(0, 2 * box_bytes),
            name="sums",
        )(slots, returned, *received)

    return (input_gradient_rows, grad_down_t.transpose(0, 2, 1), grad_up)


def solution(mesh):
    in_specs = (
        P(("fsdp", "dp"), None),
        P(("fsdp", "dp"), None),
        P("fsdp", None),
        P("dp", "fsdp", None),
        P("dp", "fsdp", None),
        P(("fsdp", "dp")),
        P(),
    )
    out_specs = (P(("fsdp", "dp"), None), P("dp", "fsdp", None), P("dp", "fsdp", None))
    return jax.shard_map(
        on_device, mesh=mesh, in_specs=in_specs, out_specs=out_specs, check_vma=False
    )
```

```python
import functools
import math

import jax
import jax.numpy as jnp
from jax import lax
from jax.experimental import pallas as pl
from jax.experimental.pallas import tpu as pltpu
from jax.sharding import PartitionSpec as P

adapter_scale_factor = 2.0
lanes = 128
base_weight = 10
store_parts = 4
BF16, F32 = jnp.bfloat16, jnp.float32
NT = (((1,), (1,)), ((), ()))
TN = (((0,), (0,)), ((), ()))
NN = (((1,), (0,)), ((), ()))


def params():
    return pltpu.CompilerParams(vmem_limit_bytes=40 * 1024 * 1024)


def cost(flops, nbytes):
    return pl.CostEstimate(flops=flops, bytes_accessed=nbytes, transcendentals=0)


def dot(a, b, dims):
    return lax.dot_general(a, b, dims, preferred_element_type=F32)


def packed_rows(kv_rows):
    if kv_rows % 32 == 0:
        return kv_rows // 2, 2
    return -(-kv_rows // 16) * 16, 1


def pack_up(block):
    kv_rows, rank = block.shape
    rows, groups = packed_rows(kv_rows)
    if groups == 2:
        return jnp.concatenate([block[:rows], block[rows:]], axis=1)
    block = jnp.concatenate([block, jnp.zeros((kv_rows, lanes - rank), block.dtype)], axis=1)
    if rows == kv_rows:
        return block
    return jnp.concatenate([block, jnp.zeros((rows - kv_rows, lanes), block.dtype)], axis=0)


def unpack_up(packed, kv_rows, rank):
    rows, groups = packed_rows(kv_rows)
    if groups == 2:
        return jnp.concatenate([packed[:, :rank], packed[:, rank:]], axis=0)
    return packed[:kv_rows, :rank]


def wide(ref, index, first, count, rank):
    return jnp.concatenate(
        [
            ref[index, pl.ds(pl.multiple_of((first + j) * rank, 16), rank), :]
            for j in range(count)
        ],
        axis=1,
    )


def select_kernel(dp_count, slots, *refs):
    downs, ups, (out, held, sems) = (
        refs[:dp_count], refs[dp_count : 2 * dp_count], refs[2 * dp_count :],
    )
    own, rank, rows = downs[0].shape
    here = lax.axis_index("dp")
    cut = rows // lanes * rank

    @pl.loop(0, out.shape[0])
    def _(k):
        place = slots[k] % own
        step = (slots[k] // own) ^ here
        for j in range(dp_count):

            @pl.when(step == j)
            def _():
                for c in range(rows // lanes):
                    held[k, c * rank : (c + 1) * rank, :] = downs[j][
                        place, :, c * lanes : (c + 1) * lanes
                    ]
                held[k, cut:, :] = pack_up(ups[j][place])

        pltpu.make_async_copy(held.at[k], out.at[k], sems.at[k]).start()

    @pl.loop(0, out.shape[0])
    def _(k):
        pltpu.make_async_copy(held.at[k], out.at[k], sems.at[k]).wait()


def middle_kernel(kv_rows, rank, halves, x, g, got, hidden_out, back, out, up_out, sems):
    fsdp_count = got.shape[0]
    tiles = x.shape[1] // fsdp_count // lanes
    rows = tiles * lanes
    cut = tiles * rank
    up = jnp.concatenate(
        [unpack_up(got[f, cut:, :], kv_rows, rank) for f in range(fsdp_count)], axis=0
    )
    hidden = dot(g[...], up, NN).astype(BF16)
    hidden_out[...] = hidden
    inner = jnp.zeros((x.shape[0], rank), F32)
    stores = []
    step = max(1, fsdp_count // store_parts)
    for f in range(fsdp_count):
        x_part = x[:, f * rows : (f + 1) * rows]
        inner += dot(x_part, wide(got, f, 0, tiles, rank), NT)
        down = (adapter_scale_factor * dot(hidden, x_part, TN)).astype(BF16)
        for c in range(tiles):
            half, at = c * halves // tiles, c % (tiles // halves) * rank
            out[f * halves + half, at : at + rank, :] = down[:, c * lanes : (c + 1) * lanes]
        if (f + 1) % step == 0:
            here = pl.ds((f + 1 - step) * halves, step * halves)
            stores.append(
                pltpu.make_async_copy(
                    out.at[here], back.at[here, 0 : out.shape[1], :], sems.at[len(stores)]
                )
            )
            stores[-1].start()
    part_up = (adapter_scale_factor * dot(g[...], inner.astype(BF16), TN)).astype(BF16)
    for f in range(fsdp_count):
        packed = pack_up(part_up[f * kv_rows : (f + 1) * kv_rows])
        for half in range(halves):
            up_out[f * halves + half] = packed
    stores.append(
        pltpu.make_async_copy(
            up_out,
            back.at[:, out.shape[1] : out.shape[1] + up_out.shape[1], :],
            sems.at[len(stores)],
        )
    )
    stores[-1].start()
    for store in stores:
        store.wait()


def base_kernel(rels, near_count, layers, own, *refs):
    near, refs = refs[:near_count], refs[near_count:]
    outs, refs = refs[-len(rels) :], refs[: -len(rels)]
    ws, near_other, others = (
        refs[: 2 * layers],
        refs[2 * layers : 2 * layers + near_count],
        refs[2 * layers + near_count :],
    )
    tokens = own.shape[0]
    cols = ws[0].shape[0]
    here = [w[...] for w in ws]
    beside = [ref[tokens:, :] for pair in zip(near, near_other) for ref in pair]
    gs = [own[...]] + [ref[:tokens, :] for ref in near]
    gs += [
        ref[n * tokens : (n + 1) * tokens, :] for ref in others for n in range(near_count + 1)
    ]
    for (i, _), g, out in zip(rels, gs, outs):
        if i == 0:
            parts = here + beside
        else:
            parts = here[1:layers] + here[layers + 1 :]
        for k, w in enumerate(parts):
            out[:, k * cols : (k + 1) * cols] = dot(g, w, NT).astype(BF16)


def out_kernel(rels, layers, inner_count, split, rows, rank, hidden, got, *refs):
    pieces, out = refs[:-1], refs[-1]
    f_here = lax.axis_index("fsdp")
    d_here = lax.axis_index("dp") % split
    cols = rows // split
    tiles = cols // lanes
    h = hidden[...]
    far = [k * inner_count + core for core in range(2) for k in range(1, layers)]
    every = [k * inner_count + core for core in range(2) for k in range(layers)]
    every += [i + core for i in range(2, inner_count, 2) for core in range(2)]
    for (i_rel, d_rel), piece in zip(rels, pieces):
        d = d_here ^ d_rel
        for k, f_rel in enumerate(every if i_rel == 0 else far):
            f = f_here ^ (f_rel ^ i_rel)
            low = adapter_scale_factor * dot(h, wide(got, f, d * tiles, tiles, rank), NN)
            start = pl.multiple_of(f * rows + d * cols, lanes)
            out[:, pl.ds(start, cols)] = (
                piece[:, k * cols : (k + 1) * cols].astype(F32) + low
            ).astype(BF16)


def sort_kernel(dp_count, own, slots, got, *sends):
    here = lax.axis_index("dp")

    @pl.loop(0, got.shape[0])
    def _(k):
        slot = slots[k]
        place = slot % own
        step = (slot // own) ^ here
        for j in range(1, dp_count):

            @pl.when(step == j)
            def _():
                sends[j - 1][place] = got[k]


def sum_kernel(dp_count, kv_rows, slots, got, *refs):
    received, (down, up) = refs[: dp_count - 1], refs[dp_count - 1 :]
    own, rank, rows = down.shape
    here = lax.axis_index("dp")
    tiles = rows // lanes

    @pl.loop(0, got.shape[0])
    def _(k):
        slot = slots[k]
        place = slot % own

        @pl.when(slot // own == here)
        def _():
            total = got[k].astype(F32)
            for ref in received:
                total += ref[place].astype(F32)
            total = total.astype(BF16)
            for c in range(tiles):
                down[place, :, c * lanes : (c + 1) * lanes] = total[c * rank : (c + 1) * rank]
            up[place] = unpack_up(total[tiles * rank :], kv_rows, rank)


def sum_halves_kernel(dp_count, kv_rows, first, steps, *refs):
    slots, got, outs, place_of = refs[:dp_count], refs[dp_count], refs[dp_count + 1 : -1], refs[-1]
    own, rank, width = outs[0].shape
    tiles = width // lanes
    here = lax.axis_index("dp")

    @pl.loop(0, slots[0].shape[0])
    def _(k):
        for j in range(dp_count):
            place_of[j, slots[j][k]] = k * dp_count + (here ^ j)

    for step, out in zip(range(first, first + steps), outs):

        @pl.loop(0, own)
        def _(place):
            slot = (here ^ step) * own + place
            total = got[place_of[0, slot]].astype(F32)
            for j in range(1, dp_count):
                total += got[place_of[j, slot]].astype(F32)
            total = total.astype(BF16)
            for c in range(tiles):
                out[place, :, c * lanes : (c + 1) * lanes] = total[c * rank : (c + 1) * rank]
            if step == 0:
                outs[-1][place] = unpack_up(total[tiles * rank :], kv_rows, rank)


def join_kernel(dp_count, *refs):
    parts, out = refs[:-1], refs[-1]
    width = parts[0].shape[2]
    here = lax.axis_index("dp")
    for step, part in enumerate(parts):
        out[:, :, pl.ds(pl.multiple_of((here ^ step) * width, lanes), width)] = part[...]


def vmem(count):
    return [pl.BlockSpec(memory_space=pltpu.VMEM)] * count


def smem(count):
    return [pl.BlockSpec(memory_space=pltpu.SMEM)] * count


def bits(count):
    return [1 << n for n in range(count.bit_length() - 1)]


def axis_count(axis):
    names = (axis,) if isinstance(axis, str) else axis
    return math.prod(lax.axis_size(name) for name in names)


def exchange(name, array, axis, bits):
    with jax.named_scope(name):
        return lax.ppermute(array, axis, xor_pairs(axis_count(axis), bits))


def xor_pairs(count, bits):
    return [(n, n ^ bits) for n in range(count)]


def on_device(inputs, grad_value, w_value, adapter_down, adapter_up, tenant_ids, slot_table):
    tokens, width = inputs.shape
    kv_width = grad_value.shape[1]
    own, rows, rank = adapter_down.shape
    kv_rows = adapter_up.shape[1]
    fsdp_count = lax.axis_size("fsdp")
    dp_count = lax.axis_size("dp")
    inner_count = 1
    while inner_count * inner_count < fsdp_count:
        inner_count *= 2
    layers = fsdp_count // inner_count
    split = 1
    while split * 2 <= dp_count and rows // (split * 2) >= lanes:
        split *= 2
    cols = rows // split
    tall = rows // lanes * rank + packed_rows(kv_rows)[0]

    down_t = adapter_down.transpose(0, 2, 1)
    downs, ups = [down_t], [adapter_up]
    for j in range(1, dp_count):
        downs.append(exchange("down_dp", down_t, "dp", j))
        ups.append(exchange("up_dp", adapter_up, "dp", j))
    with jax.named_scope("ids"):
        ids = lax.all_to_all(
            jnp.broadcast_to(tenant_ids[:, None, None], (fsdp_count, 1, lanes)), "fsdp", 0, 0, tiled=True
        )[:, 0, 0]

    w_here = lax.dynamic_slice_in_dim(w_value, lax.axis_index("dp") % split * cols, cols, 0)
    ws = [w_here] + [None] * (layers - 1)
    for bit in bits(layers):
        ws[bit] = exchange("w_layers", w_here, "fsdp", bit * inner_count)
    rels = [(i, 0) for i in range(0, inner_count, 2)]
    beside = jnp.concatenate([grad_value, w_here], axis=0)
    near = [exchange("g_w_layer", beside, "fsdp", i) for i, _ in rels[1:]]
    ids, downs, ups, ws, near = lax.optimization_barrier((ids, downs, ups, ws, near))
    held = jnp.concatenate([grad_value] + [n[:tokens] for n in near], axis=0)
    others = [exchange("g_dp", held, "dp", d) for d in range(1, split)]
    rels = rels + [(i, d) for d in range(1, split) for i, _ in rels]

    box = jax.ShapeDtypeStruct((fsdp_count, tall, lanes), BF16)
    box_bytes = 2 * fsdp_count * tall * lanes
    slots = jnp.sum(
        jnp.where(
            ids[:, None] == jnp.arange(slot_table.shape[0])[None, :], slot_table[None, :], 0
        ),
        axis=1,
    )
    ups[0] = pltpu.with_memory_space_constraint(ups[0], pltpu.HBM)
    downs[0] = pltpu.with_memory_space_constraint(downs[0], pltpu.HBM)
    sent = pl.pallas_call(
        functools.partial(select_kernel, dp_count),
        out_shape=pltpu.HBM(box.shape, BF16),
        in_specs=smem(1) + vmem(2 * dp_count),
        out_specs=pl.BlockSpec(memory_space=pltpu.HBM),
        scratch_shapes=[
            pltpu.VMEM(box.shape, BF16), pltpu.SemaphoreType.DMA((fsdp_count,)),
        ],
        compiler_params=params(),
        cost_estimate=cost(0, 2 * box_bytes),
        name="select",
    )(slots, *downs, *ups)
    with jax.named_scope("adapters_to_blocks"):
        got = lax.all_to_all(sent, "fsdp", 0, 0, tiled=True)
    for bit in reversed(bits(layers)):
        for k in range(0, layers, 2 * bit):
            if ws[k + bit] is None:
                ws[k + bit] = exchange("w_last", ws[k], "fsdp", bit * inner_count)
    ws = ws + [exchange("w_core", w, "fsdp", 1) for w in ws]
    near_other = [exchange("w_core", n, "fsdp", 1) for n in near]

    ws = [pltpu.with_memory_space_constraint(w, pltpu.HBM) for w in ws[:layers]] + ws[layers:]
    wide_cols = (2 * layers + 2 * len(near)) * cols
    pieces = pl.pallas_call(
        functools.partial(base_kernel, rels, len(near), layers),
        out_shape=[
            jax.ShapeDtypeStruct((tokens, wide_cols if i == 0 else (2 * layers - 2) * cols), BF16)
            for i, _ in rels
        ],
        in_specs=vmem(1 + 2 * len(near) + len(ws) + len(others)),
        out_specs=vmem(len(rels)),
        compiler_params=params(),
        cost_estimate=cost(
            base_weight * 2 * tokens * width * kv_width, base_weight * 4 * tokens * width
        ),
        name="base",
    )(grad_value, *near, *ws, *near_other, *others)
    pieces = [pieces[0]] + [
        exchange("pieces%d%d" % (i, d), p, ("fsdp", "dp"), i * dp_count + d)
        for (i, d), p in zip(rels[1:], pieces[1:])
    ]
    got, pieces[:-1] = lax.optimization_barrier((got, pieces[:-1]))

    tiles = rows // lanes
    halves = dp_count if tiles % dp_count == 0 else 1
    cut = tiles // halves * rank
    small = packed_rows(kv_rows)[0]
    back_shape = (fsdp_count * halves, cut + small, lanes)
    hidden, back = pl.pallas_call(
        functools.partial(middle_kernel, kv_rows, rank, halves),
        out_shape=[
            jax.ShapeDtypeStruct((tokens, rank), BF16),
            pltpu.HBM(back_shape, BF16),
        ],
        in_specs=vmem(3),
        out_specs=vmem(1) + [pl.BlockSpec(memory_space=pltpu.HBM)],
        scratch_shapes=[
            pltpu.VMEM((fsdp_count * halves, cut, lanes), BF16),
            pltpu.VMEM((fsdp_count * halves, small, lanes), BF16),
            pltpu.SemaphoreType.DMA((store_parts + 1,)),
        ],
        compiler_params=params(),
        cost_estimate=cost(4 * tokens * width * rank, 2 * tokens * width + 2 * box_bytes),
        name="middle",
    )(inputs, grad_value, got)
    with jax.named_scope("gradients_back"):
        axes = "fsdp" if halves == 1 else ("fsdp", "dp")
        returned = lax.all_to_all(back, axes, 0, 0, tiled=True)
    if halves > 1:
        all_slots = [slots] + [exchange("slots_dp", slots, "dp", j) for j in range(1, dp_count)]
        returned, all_slots = lax.optimization_barrier((returned, all_slots))
    returned, pieces = lax.optimization_barrier((returned, pieces))

    input_gradient_rows = pl.pallas_call(
        functools.partial(out_kernel, rels, layers, inner_count, split, rows, rank),
        out_shape=jax.ShapeDtypeStruct((tokens, width), BF16),
        in_specs=vmem(2 + len(rels)),
        out_specs=pl.BlockSpec(memory_space=pltpu.VMEM),
        compiler_params=params(),
        cost_estimate=cost(2 * tokens * width * rank, 4 * tokens * width + box_bytes),
        name="rows",
    )(hidden, got, *pieces)

    if halves > 1:
        part = (own, rank, rows // halves)

        def sum_halves(first, steps, extra, name):
            return pl.pallas_call(
                functools.partial(sum_halves_kernel, dp_count, kv_rows, first, steps),
                out_shape=[jax.ShapeDtypeStruct(shape, BF16) for shape in [part] * steps + extra],
                in_specs=smem(dp_count) + vmem(1),
                out_specs=vmem(steps + len(extra)),
                scratch_shapes=[pltpu.SMEM((dp_count, own * dp_count), jnp.int32)],
                compiler_params=params(),
                cost_estimate=cost(0, 2 * box_bytes),
                name=name,
            )(*all_slots, returned)

        *sums, grad_up = sum_halves(0, dp_count, [adapter_up.shape], "sum_all")
        received = [exchange("grads_dp", s, "dp", j) for j, s in enumerate(sums[1:], 1)]
        received, input_gradient_rows, sums[0], grad_up = lax.optimization_barrier(
            (received, input_gradient_rows, sums[0], grad_up)
        )
        grad_down_t = pl.pallas_call(
            functools.partial(join_kernel, dp_count),
            out_shape=jax.ShapeDtypeStruct((own, rank, rows), BF16),
            in_specs=vmem(dp_count),
            out_specs=pl.BlockSpec(memory_space=pltpu.VMEM),
            compiler_params=params(),
            cost_estimate=cost(0, 4 * own * rank * rows),
            name="join",
        )(sums[0], *received)
    else:
        sends = pl.pallas_call(
            functools.partial(sort_kernel, dp_count, own),
            out_shape=[jax.ShapeDtypeStruct((own, tall, lanes), BF16)] * (dp_count - 1),
            in_specs=smem(1) + vmem(1),
            out_specs=vmem(dp_count - 1),
            compiler_params=params(),
            cost_estimate=cost(0, 2 * box_bytes),
            name="sort",
        )(slots, returned)
        received = [
            exchange("grads_dp", s, "dp", j + 1) for j, s in enumerate(sends)
        ]
        received, input_gradient_rows = lax.optimization_barrier((received, input_gradient_rows))
        grad_down_t, grad_up = pl.pallas_call(
            functools.partial(sum_kernel, dp_count, kv_rows),
            out_shape=[
                jax.ShapeDtypeStruct((own, rank, rows), BF16),
                jax.ShapeDtypeStruct(adapter_up.shape, BF16),
            ],
            in_specs=smem(1) + vmem(dp_count),
            out_specs=vmem(2),
            compiler_params=params(),
            cost_estimate=cost(0, 2 * box_bytes),
            name="sums",
        )(slots, returned, *received)

    return (input_gradient_rows, grad_down_t.transpose(0, 2, 1), grad_up)


def solution(mesh):
    in_specs = (
        P(("fsdp", "dp"), None),
        P(("fsdp", "dp"), None),
        P("fsdp", None),
        P("dp", "fsdp", None),
        P("dp", "fsdp", None),
        P(("fsdp", "dp")),
        P(),
    )
    out_specs = (P(("fsdp", "dp"), None), P("dp", "fsdp", None), P("dp", "fsdp", None))
    return jax.shard_map(
        on_device, mesh=mesh, in_specs=in_specs, out_specs=out_specs, check_vma=False
    )
```

```python
import functools
import math

import jax
import jax.numpy as jnp
from jax import lax
from jax.experimental import pallas as pl
from jax.experimental.pallas import tpu as pltpu
from jax.sharding import PartitionSpec as P

adapter_scale_factor = 2.0
lanes = 128
base_weight = 10
store_parts = 4
BF16, F32 = jnp.bfloat16, jnp.float32
NT = (((1,), (1,)), ((), ()))
TN = (((0,), (0,)), ((), ()))
NN = (((1,), (0,)), ((), ()))


def params():
    return pltpu.CompilerParams(vmem_limit_bytes=40 * 1024 * 1024)


def cost(flops, nbytes):
    return pl.CostEstimate(flops=flops, bytes_accessed=nbytes, transcendentals=0)


def dot(a, b, dims):
    return lax.dot_general(a, b, dims, preferred_element_type=F32)


def packed_rows(kv_rows):
    if kv_rows % 32 == 0:
        return kv_rows // 2, 2
    return -(-kv_rows // 16) * 16, 1


def pack_up(block):
    kv_rows, rank = block.shape
    rows, groups = packed_rows(kv_rows)
    if groups == 2:
        return jnp.concatenate([block[:rows], block[rows:]], axis=1)
    block = jnp.concatenate([block, jnp.zeros((kv_rows, lanes - rank), block.dtype)], axis=1)
    if rows == kv_rows:
        return block
    return jnp.concatenate([block, jnp.zeros((rows - kv_rows, lanes), block.dtype)], axis=0)


def unpack_up(packed, kv_rows, rank):
    rows, groups = packed_rows(kv_rows)
    if groups == 2:
        return jnp.concatenate([packed[:, :rank], packed[:, rank:]], axis=0)
    return packed[:kv_rows, :rank]


def wide(ref, index, first, count, rank):
    return jnp.concatenate(
        [
            ref[index, pl.ds(pl.multiple_of((first + j) * rank, 16), rank), :]
            for j in range(count)
        ],
        axis=1,
    )


def select_kernel(dp_count, slots, *refs):
    downs, ups, (out, held, sems) = (
        refs[:dp_count], refs[dp_count : 2 * dp_count], refs[2 * dp_count :],
    )
    own, rank, rows = downs[0].shape
    here = lax.axis_index("dp")
    cut = rows // lanes * rank

    @pl.loop(0, out.shape[0])
    def _(k):
        place = slots[k] % own
        step = (slots[k] // own) ^ here
        for j in range(dp_count):

            @pl.when(step == j)
            def _():
                for c in range(rows // lanes):
                    held[k, c * rank : (c + 1) * rank, :] = downs[j][
                        place, :, c * lanes : (c + 1) * lanes
                    ]
                held[k, cut:, :] = pack_up(ups[j][place])

        pltpu.make_async_copy(held.at[k], out.at[k], sems.at[k]).start()

    @pl.loop(0, out.shape[0])
    def _(k):
        pltpu.make_async_copy(held.at[k], out.at[k], sems.at[k]).wait()


def middle_kernel(kv_rows, rank, halves, x, g, got, hidden_out, back, out, up_out, sems):
    fsdp_count = got.shape[0]
    tiles = x.shape[1] // fsdp_count // lanes
    rows = tiles * lanes
    cut = tiles * rank
    up = jnp.concatenate(
        [unpack_up(got[f, cut:, :], kv_rows, rank) for f in range(fsdp_count)], axis=0
    )
    hidden = dot(g[...], up, NN).astype(BF16)
    hidden_out[...] = hidden
    inner = jnp.zeros((x.shape[0], rank), F32)
    stores = []
    step = max(1, fsdp_count // store_parts)
    for f in range(fsdp_count):
        x_part = x[:, f * rows : (f + 1) * rows]
        inner += dot(x_part, wide(got, f, 0, tiles, rank), NT)
        down = (adapter_scale_factor * dot(hidden, x_part, TN)).astype(BF16)
        for c in range(tiles):
            half, at = c * halves // tiles, c % (tiles // halves) * rank
            out[f * halves + half, at : at + rank, :] = down[:, c * lanes : (c + 1) * lanes]
        if (f + 1) % step == 0:
            here = pl.ds((f + 1 - step) * halves, step * halves)
            stores.append(
                pltpu.make_async_copy(
                    out.at[here], back.at[here, 0 : out.shape[1], :], sems.at[len(stores)]
                )
            )
            stores[-1].start()
    part_up = (adapter_scale_factor * dot(g[...], inner.astype(BF16), TN)).astype(BF16)
    for f in range(fsdp_count):
        packed = pack_up(part_up[f * kv_rows : (f + 1) * kv_rows])
        for half in range(halves):
            up_out[f * halves + half] = packed
    stores.append(
        pltpu.make_async_copy(
            up_out,
            back.at[:, out.shape[1] : out.shape[1] + up_out.shape[1], :],
            sems.at[len(stores)],
        )
    )
    stores[-1].start()
    for store in stores:
        store.wait()


def base_kernel(rels, near_count, layers, own, *refs):
    near, refs = refs[:near_count], refs[near_count:]
    outs, refs = refs[-len(rels) :], refs[: -len(rels)]
    ws, near_other, others = (
        refs[: 2 * layers],
        refs[2 * layers : 2 * layers + near_count],
        refs[2 * layers + near_count :],
    )
    tokens = own.shape[0]
    cols = ws[0].shape[0]
    here = [w[...] for w in ws]
    beside = [ref[tokens:, :] for pair in zip(near, near_other) for ref in pair]
    gs = [own[...]] + [ref[:tokens, :] for ref in near]
    gs += [
        ref[n * tokens : (n + 1) * tokens, :] for ref in others for n in range(near_count + 1)
    ]
    for (i, _), g, out in zip(rels, gs, outs):
        if i == 0:
            parts = here + beside
        else:
            parts = here[1:layers] + here[layers + 1 :]
        for k, w in enumerate(parts):
            out[:, k * cols : (k + 1) * cols] = dot(g, w, NT).astype(BF16)


def out_kernel(rels, layers, inner_count, split, rows, rank, hidden, got, *refs):
    pieces, out = refs[:-1], refs[-1]
    f_here = lax.axis_index("fsdp")
    d_here = lax.axis_index("dp") % split
    cols = rows // split
    tiles = cols // lanes
    h = hidden[...]
    far = [k * inner_count + core for core in range(2) for k in range(1, layers)]
    every = [k * inner_count + core for core in range(2) for k in range(layers)]
    every += [i + core for i in range(2, inner_count, 2) for core in range(2)]
    for (i_rel, d_rel), piece in zip(rels, pieces):
        d = d_here ^ d_rel
        for k, f_rel in enumerate(every if i_rel == 0 else far):
            f = f_here ^ (f_rel ^ i_rel)
            low = adapter_scale_factor * dot(h, wide(got, f, d * tiles, tiles, rank), NN)
            start = pl.multiple_of(f * rows + d * cols, lanes)
            out[:, pl.ds(start, cols)] = (
                piece[:, k * cols : (k + 1) * cols].astype(F32) + low
            ).astype(BF16)


def sort_kernel(dp_count, own, slots, got, *sends):
    here = lax.axis_index("dp")

    @pl.loop(0, got.shape[0])
    def _(k):
        slot = slots[k]
        place = slot % own
        step = (slot // own) ^ here
        for j in range(1, dp_count):

            @pl.when(step == j)
            def _():
                sends[j - 1][place] = got[k]


def sum_kernel(dp_count, kv_rows, slots, got, *refs):
    received, (down, up) = refs[: dp_count - 1], refs[dp_count - 1 :]
    own, rank, rows = down.shape
    here = lax.axis_index("dp")
    tiles = rows // lanes

    @pl.loop(0, got.shape[0])
    def _(k):
        slot = slots[k]
        place = slot % own

        @pl.when(slot // own == here)
        def _():
            total = got[k].astype(F32)
            for ref in received:
                total += ref[place].astype(F32)
            total = total.astype(BF16)
            for c in range(tiles):
                down[place, :, c * lanes : (c + 1) * lanes] = total[c * rank : (c + 1) * rank]
            up[place] = unpack_up(total[tiles * rank :], kv_rows, rank)


def sum_halves_kernel(dp_count, kv_rows, first, steps, *refs):
    slots, got, outs, place_of = refs[:dp_count], refs[dp_count], refs[dp_count + 1 : -1], refs[-1]
    own, rank, width = outs[0].shape
    tiles = width // lanes
    here = lax.axis_index("dp")

    @pl.loop(0, slots[0].shape[0], unroll=4)
    def _(k):
        for j in range(dp_count):
            place_of[j, slots[j][k]] = k * dp_count + (here ^ j)

    for step, out in zip(range(first, first + steps), outs):

        @pl.loop(0, own, unroll=4)
        def _(place):
            slot = (here ^ step) * own + place
            total = got[place_of[0, slot]].astype(F32)
            for j in range(1, dp_count):
                total += got[place_of[j, slot]].astype(F32)
            total = total.astype(BF16)
            for c in range(tiles):
                out[place, :, c * lanes : (c + 1) * lanes] = total[c * rank : (c + 1) * rank]
            if step == 0:
                outs[-1][place] = unpack_up(total[tiles * rank :], kv_rows, rank)


def join_kernel(dp_count, *refs):
    parts, out = refs[:-1], refs[-1]
    width = parts[0].shape[2]
    here = lax.axis_index("dp")
    for step, part in enumerate(parts):
        out[:, :, pl.ds(pl.multiple_of((here ^ step) * width, lanes), width)] = part[...]


def vmem(count):
    return [pl.BlockSpec(memory_space=pltpu.VMEM)] * count


def smem(count):
    return [pl.BlockSpec(memory_space=pltpu.SMEM)] * count


def bits(count):
    return [1 << n for n in range(count.bit_length() - 1)]


def axis_count(axis):
    names = (axis,) if isinstance(axis, str) else axis
    return math.prod(lax.axis_size(name) for name in names)


def exchange(name, array, axis, bits):
    with jax.named_scope(name):
        return lax.ppermute(array, axis, xor_pairs(axis_count(axis), bits))


def xor_pairs(count, bits):
    return [(n, n ^ bits) for n in range(count)]


def on_device(inputs, grad_value, w_value, adapter_down, adapter_up, tenant_ids, slot_table):
    tokens, width = inputs.shape
    kv_width = grad_value.shape[1]
    own, rows, rank = adapter_down.shape
    kv_rows = adapter_up.shape[1]
    fsdp_count = lax.axis_size("fsdp")
    dp_count = lax.axis_size("dp")
    inner_count = 1
    while inner_count * inner_count < fsdp_count:
        inner_count *= 2
    layers = fsdp_count // inner_count
    split = 1
    while split * 2 <= dp_count and rows // (split * 2) >= lanes:
        split *= 2
    cols = rows // split
    tall = rows // lanes * rank + packed_rows(kv_rows)[0]

    down_t = adapter_down.transpose(0, 2, 1)
    downs, ups = [down_t], [adapter_up]
    for j in range(1, dp_count):
        downs.append(exchange("down_dp", down_t, "dp", j))
        ups.append(exchange("up_dp", adapter_up, "dp", j))
    with jax.named_scope("ids"):
        ids = lax.all_to_all(
            jnp.broadcast_to(tenant_ids[:, None, None], (fsdp_count, 1, lanes)), "fsdp", 0, 0, tiled=True
        )[:, 0, 0]

    w_here = lax.dynamic_slice_in_dim(w_value, lax.axis_index("dp") % split * cols, cols, 0)
    ws = [w_here] + [None] * (layers - 1)
    for bit in bits(layers):
        ws[bit] = exchange("w_layers", w_here, "fsdp", bit * inner_count)
    rels = [(i, 0) for i in range(0, inner_count, 2)]
    beside = jnp.concatenate([grad_value, w_here], axis=0)
    near = [exchange("g_w_layer", beside, "fsdp", i) for i, _ in rels[1:]]
    ids, downs, ups, ws, near = lax.optimization_barrier((ids, downs, ups, ws, near))
    held = jnp.concatenate([grad_value] + [n[:tokens] for n in near], axis=0)
    others = [exchange("g_dp", held, "dp", d) for d in range(1, split)]
    rels = rels + [(i, d) for d in range(1, split) for i, _ in rels]

    box = jax.ShapeDtypeStruct((fsdp_count, tall, lanes), BF16)
    box_bytes = 2 * fsdp_count * tall * lanes
    slots = jnp.sum(
        jnp.where(
            ids[:, None] == jnp.arange(slot_table.shape[0])[None, :], slot_table[None, :], 0
        ),
        axis=1,
    )
    ups[0] = pltpu.with_memory_space_constraint(ups[0], pltpu.HBM)
    downs[0] = pltpu.with_memory_space_constraint(downs[0], pltpu.HBM)
    sent = pl.pallas_call(
        functools.partial(select_kernel, dp_count),
        out_shape=pltpu.HBM(box.shape, BF16),
        in_specs=smem(1) + vmem(2 * dp_count),
        out_specs=pl.BlockSpec(memory_space=pltpu.HBM),
        scratch_shapes=[
            pltpu.VMEM(box.shape, BF16), pltpu.SemaphoreType.DMA((fsdp_count,)),
        ],
        compiler_params=params(),
        cost_estimate=cost(0, 2 * box_bytes),
        name="select",
    )(slots, *downs, *ups)
    with jax.named_scope("adapters_to_blocks"):
        got = lax.all_to_all(sent, "fsdp", 0, 0, tiled=True)
    for bit in reversed(bits(layers)):
        for k in range(0, layers, 2 * bit):
            if ws[k + bit] is None:
                ws[k + bit] = exchange("w_last", ws[k], "fsdp", bit * inner_count)
    ws = ws + [exchange("w_core", w, "fsdp", 1) for w in ws]
    near_other = [exchange("w_core", n, "fsdp", 1) for n in near]

    ws = [pltpu.with_memory_space_constraint(w, pltpu.HBM) for w in ws[:layers]] + ws[layers:]
    wide_cols = (2 * layers + 2 * len(near)) * cols
    pieces = pl.pallas_call(
        functools.partial(base_kernel, rels, len(near), layers),
        out_shape=[
            jax.ShapeDtypeStruct((tokens, wide_cols if i == 0 else (2 * layers - 2) * cols), BF16)
            for i, _ in rels
        ],
        in_specs=vmem(1 + 2 * len(near) + len(ws) + len(others)),
        out_specs=vmem(len(rels)),
        compiler_params=params(),
        cost_estimate=cost(
            base_weight * 2 * tokens * width * kv_width, base_weight * 4 * tokens * width
        ),
        name="base",
    )(grad_value, *near, *ws, *near_other, *others)
    pieces = [pieces[0]] + [
        exchange("pieces%d%d" % (i, d), p, ("fsdp", "dp"), i * dp_count + d)
        for (i, d), p in zip(rels[1:], pieces[1:])
    ]
    got, pieces[:-1] = lax.optimization_barrier((got, pieces[:-1]))

    tiles = rows // lanes
    halves = dp_count if tiles % dp_count == 0 else 1
    cut = tiles // halves * rank
    small = packed_rows(kv_rows)[0]
    back_shape = (fsdp_count * halves, cut + small, lanes)
    hidden, back = pl.pallas_call(
        functools.partial(middle_kernel, kv_rows, rank, halves),
        out_shape=[
            jax.ShapeDtypeStruct((tokens, rank), BF16),
            pltpu.HBM(back_shape, BF16),
        ],
        in_specs=vmem(3),
        out_specs=vmem(1) + [pl.BlockSpec(memory_space=pltpu.HBM)],
        scratch_shapes=[
            pltpu.VMEM((fsdp_count * halves, cut, lanes), BF16),
            pltpu.VMEM((fsdp_count * halves, small, lanes), BF16),
            pltpu.SemaphoreType.DMA((store_parts + 1,)),
        ],
        compiler_params=params(),
        cost_estimate=cost(4 * tokens * width * rank, 2 * tokens * width + 2 * box_bytes),
        name="middle",
    )(inputs, grad_value, got)
    with jax.named_scope("gradients_back"):
        axes = "fsdp" if halves == 1 else ("fsdp", "dp")
        returned = lax.all_to_all(back, axes, 0, 0, tiled=True)
    if halves > 1:
        all_slots = [slots] + [exchange("slots_dp", slots, "dp", j) for j in range(1, dp_count)]
        returned, all_slots = lax.optimization_barrier((returned, all_slots))
    returned, pieces = lax.optimization_barrier((returned, pieces))

    input_gradient_rows = pl.pallas_call(
        functools.partial(out_kernel, rels, layers, inner_count, split, rows, rank),
        out_shape=jax.ShapeDtypeStruct((tokens, width), BF16),
        in_specs=vmem(2 + len(rels)),
        out_specs=pl.BlockSpec(memory_space=pltpu.VMEM),
        compiler_params=params(),
        cost_estimate=cost(2 * tokens * width * rank, 4 * tokens * width + box_bytes),
        name="rows",
    )(hidden, got, *pieces)

    if halves > 1:
        part = (own, rank, rows // halves)

        def sum_halves(first, steps, extra, name):
            return pl.pallas_call(
                functools.partial(sum_halves_kernel, dp_count, kv_rows, first, steps),
                out_shape=[jax.ShapeDtypeStruct(shape, BF16) for shape in [part] * steps + extra],
                in_specs=smem(dp_count) + vmem(1),
                out_specs=vmem(steps + len(extra)),
                scratch_shapes=[pltpu.SMEM((dp_count, own * dp_count), jnp.int32)],
                compiler_params=params(),
                cost_estimate=cost(0, 2 * box_bytes),
                name=name,
            )(*all_slots, returned)

        *sums, grad_up = sum_halves(0, dp_count, [adapter_up.shape], "sum_all")
        received = [exchange("grads_dp", s, "dp", j) for j, s in enumerate(sums[1:], 1)]
        received, input_gradient_rows, sums[0], grad_up = lax.optimization_barrier(
            (received, input_gradient_rows, sums[0], grad_up)
        )
        grad_down_t = pl.pallas_call(
            functools.partial(join_kernel, dp_count),
            out_shape=jax.ShapeDtypeStruct((own, rank, rows), BF16),
            in_specs=vmem(dp_count),
            out_specs=pl.BlockSpec(memory_space=pltpu.VMEM),
            compiler_params=params(),
            cost_estimate=cost(0, 4 * own * rank * rows),
            name="join",
        )(sums[0], *received)
    else:
        sends = pl.pallas_call(
            functools.partial(sort_kernel, dp_count, own),
            out_shape=[jax.ShapeDtypeStruct((own, tall, lanes), BF16)] * (dp_count - 1),
            in_specs=smem(1) + vmem(1),
            out_specs=vmem(dp_count - 1),
            compiler_params=params(),
            cost_estimate=cost(0, 2 * box_bytes),
            name="sort",
        )(slots, returned)
        received = [
            exchange("grads_dp", s, "dp", j + 1) for j, s in enumerate(sends)
        ]
        received, input_gradient_rows = lax.optimization_barrier((received, input_gradient_rows))
        grad_down_t, grad_up = pl.pallas_call(
            functools.partial(sum_kernel, dp_count, kv_rows),
            out_shape=[
                jax.ShapeDtypeStruct((own, rank, rows), BF16),
                jax.ShapeDtypeStruct(adapter_up.shape, BF16),
            ],
            in_specs=smem(1) + vmem(dp_count),
            out_specs=vmem(2),
            compiler_params=params(),
            cost_estimate=cost(0, 2 * box_bytes),
            name="sums",
        )(slots, returned, *received)

    return (input_gradient_rows, grad_down_t.transpose(0, 2, 1), grad_up)


def solution(mesh):
    in_specs = (
        P(("fsdp", "dp"), None),
        P(("fsdp", "dp"), None),
        P("fsdp", None),
        P("dp", "fsdp", None),
        P("dp", "fsdp", None),
        P(("fsdp", "dp")),
        P(),
    )
    out_specs = (P(("fsdp", "dp"), None), P("dp", "fsdp", None), P("dp", "fsdp", None))
    return jax.shard_map(
        on_device, mesh=mesh, in_specs=in_specs, out_specs=out_specs, check_vma=False
    )
```

```python
import functools
import math

import jax
import jax.numpy as jnp
from jax import lax
from jax.experimental import pallas as pl
from jax.experimental.pallas import tpu as pltpu
from jax.sharding import PartitionSpec as P

adapter_scale_factor = 2.0
lanes = 128
base_weight = 10
store_parts = 4
BF16, F32 = jnp.bfloat16, jnp.float32
NT = (((1,), (1,)), ((), ()))
TN = (((0,), (0,)), ((), ()))
NN = (((1,), (0,)), ((), ()))


def params():
    return pltpu.CompilerParams(vmem_limit_bytes=40 * 1024 * 1024)


def cost(flops, nbytes):
    return pl.CostEstimate(flops=flops, bytes_accessed=nbytes, transcendentals=0)


def dot(a, b, dims):
    return lax.dot_general(a, b, dims, preferred_element_type=F32)


def packed_rows(kv_rows):
    if kv_rows % 32 == 0:
        return kv_rows // 2, 2
    return -(-kv_rows // 16) * 16, 1


def pack_up(block):
    kv_rows, rank = block.shape
    rows, groups = packed_rows(kv_rows)
    if groups == 2:
        return jnp.concatenate([block[:rows], block[rows:]], axis=1)
    block = jnp.concatenate([block, jnp.zeros((kv_rows, lanes - rank), block.dtype)], axis=1)
    if rows == kv_rows:
        return block
    return jnp.concatenate([block, jnp.zeros((rows - kv_rows, lanes), block.dtype)], axis=0)


def unpack_up(packed, kv_rows, rank):
    rows, groups = packed_rows(kv_rows)
    if groups == 2:
        return jnp.concatenate([packed[:, :rank], packed[:, rank:]], axis=0)
    return packed[:kv_rows, :rank]


def wide(ref, index, first, count, rank):
    return jnp.concatenate(
        [
            ref[index, pl.ds(pl.multiple_of((first + j) * rank, 16), rank), :]
            for j in range(count)
        ],
        axis=1,
    )


def select_kernel(dp_count, slots, *refs):
    downs, ups, (out, held, sems) = (
        refs[:dp_count], refs[dp_count : 2 * dp_count], refs[2 * dp_count :],
    )
    own, rank, rows = downs[0].shape
    here = lax.axis_index("dp")
    cut = rows // lanes * rank

    @pl.loop(0, out.shape[0])
    def _(k):
        place = slots[k] % own
        step = (slots[k] // own) ^ here
        for j in range(dp_count):

            @pl.when(step == j)
            def _():
                for c in range(rows // lanes):
                    held[k, c * rank : (c + 1) * rank, :] = downs[j][
                        place, :, c * lanes : (c + 1) * lanes
                    ]
                held[k, cut:, :] = pack_up(ups[j][place])

        pltpu.make_async_copy(held.at[k], out.at[k], sems.at[k]).start()

    @pl.loop(0, out.shape[0])
    def _(k):
        pltpu.make_async_copy(held.at[k], out.at[k], sems.at[k]).wait()


def middle_kernel(kv_rows, rank, halves, x, g, got, hidden_out, back, out, up_out, sems):
    fsdp_count = got.shape[0]
    tiles = x.shape[1] // fsdp_count // lanes
    rows = tiles * lanes
    cut = tiles * rank
    up = jnp.concatenate(
        [unpack_up(got[f, cut:, :], kv_rows, rank) for f in range(fsdp_count)], axis=0
    )
    hidden = dot(g[...], up, NN).astype(BF16) * adapter_scale_factor
    hidden_out[...] = hidden
    inner = jnp.zeros((x.shape[0], rank), F32)
    stores = []
    step = max(1, fsdp_count // store_parts)
    for f in range(fsdp_count):
        x_part = x[:, f * rows : (f + 1) * rows]
        inner += dot(x_part, wide(got, f, 0, tiles, rank), NT)
        down = dot(hidden, x_part, TN).astype(BF16)
        for c in range(tiles):
            half, at = c * halves // tiles, c % (tiles // halves) * rank
            out[f * halves + half, at : at + rank, :] = down[:, c * lanes : (c + 1) * lanes]
        if (f + 1) % step == 0:
            here = pl.ds((f + 1 - step) * halves, step * halves)
            stores.append(
                pltpu.make_async_copy(
                    out.at[here], back.at[here, 0 : out.shape[1], :], sems.at[len(stores)]
                )
            )
            stores[-1].start()
    part_up = dot(g[...], inner.astype(BF16) * adapter_scale_factor, TN).astype(BF16)
    for f in range(fsdp_count):
        packed = pack_up(part_up[f * kv_rows : (f + 1) * kv_rows])
        for half in range(halves):
            up_out[f * halves + half] = packed
    stores.append(
        pltpu.make_async_copy(
            up_out,
            back.at[:, out.shape[1] : out.shape[1] + up_out.shape[1], :],
            sems.at[len(stores)],
        )
    )
    stores[-1].start()
    for store in stores:
        store.wait()


def base_kernel(rels, near_count, layers, own, *refs):
    near, refs = refs[:near_count], refs[near_count:]
    outs, refs = refs[-len(rels) :], refs[: -len(rels)]
    ws, near_other, others = (
        refs[: 2 * layers],
        refs[2 * layers : 2 * layers + near_count],
        refs[2 * layers + near_count :],
    )
    tokens = own.shape[0]
    cols = ws[0].shape[0]
    here = [w[...] for w in ws]
    beside = [ref[tokens:, :] for pair in zip(near, near_other) for ref in pair]
    gs = [own[...]] + [ref[:tokens, :] for ref in near]
    gs += [
        ref[n * tokens : (n + 1) * tokens, :] for ref in others for n in range(near_count + 1)
    ]
    for (i, _), g, out in zip(rels, gs, outs):
        if i == 0:
            parts = here + beside
        else:
            parts = here[1:layers] + here[layers + 1 :]
        for k, w in enumerate(parts):
            out[:, k * cols : (k + 1) * cols] = dot(g, w, NT).astype(BF16)


def out_kernel(rels, layers, inner_count, split, rows, rank, hidden, got, *refs):
    pieces, out = refs[:-1], refs[-1]
    f_here = lax.axis_index("fsdp")
    d_here = lax.axis_index("dp") % split
    cols = rows // split
    tiles = cols // lanes
    h = hidden[...]
    far = [k * inner_count + core for core in range(2) for k in range(1, layers)]
    every = [k * inner_count + core for core in range(2) for k in range(layers)]
    every += [i + core for i in range(2, inner_count, 2) for core in range(2)]
    for (i_rel, d_rel), piece in zip(rels, pieces):
        d = d_here ^ d_rel
        for k, f_rel in enumerate(every if i_rel == 0 else far):
            f = f_here ^ (f_rel ^ i_rel)
            low = dot(h, wide(got, f, d * tiles, tiles, rank), NN)
            start = pl.multiple_of(f * rows + d * cols, lanes)
            out[:, pl.ds(start, cols)] = (
                piece[:, k * cols : (k + 1) * cols].astype(F32) + low
            ).astype(BF16)


def sort_kernel(dp_count, own, slots, got, *sends):
    here = lax.axis_index("dp")

    @pl.loop(0, got.shape[0])
    def _(k):
        slot = slots[k]
        place = slot % own
        step = (slot // own) ^ here
        for j in range(1, dp_count):

            @pl.when(step == j)
            def _():
                sends[j - 1][place] = got[k]


def sum_kernel(dp_count, kv_rows, slots, got, *refs):
    received, (down, up) = refs[: dp_count - 1], refs[dp_count - 1 :]
    own, rank, rows = down.shape
    here = lax.axis_index("dp")
    tiles = rows // lanes

    @pl.loop(0, got.shape[0])
    def _(k):
        slot = slots[k]
        place = slot % own

        @pl.when(slot // own == here)
        def _():
            total = got[k].astype(F32)
            for ref in received:
                total += ref[place].astype(F32)
            total = total.astype(BF16)
            for c in range(tiles):
                down[place, :, c * lanes : (c + 1) * lanes] = total[c * rank : (c + 1) * rank]
            up[place] = unpack_up(total[tiles * rank :], kv_rows, rank)


def sum_halves_kernel(dp_count, kv_rows, first, steps, *refs):
    slots, got, outs, place_of = refs[:dp_count], refs[dp_count], refs[dp_count + 1 : -1], refs[-1]
    own, rank, width = outs[0].shape
    tiles = width // lanes
    here = lax.axis_index("dp")

    @pl.loop(0, slots[0].shape[0], unroll=4)
    def _(k):
        for j in range(dp_count):
            place_of[j, slots[j][k]] = k * dp_count + (here ^ j)

    for step, out in zip(range(first, first + steps), outs):

        @pl.loop(0, own, unroll=4)
        def _(place):
            slot = (here ^ step) * own + place
            total = got[place_of[0, slot]].astype(F32)
            for j in range(1, dp_count):
                total += got[place_of[j, slot]].astype(F32)
            total = total.astype(BF16)
            for c in range(tiles):
                out[place, :, c * lanes : (c + 1) * lanes] = total[c * rank : (c + 1) * rank]
            if step == 0:
                outs[-1][place] = unpack_up(total[tiles * rank :], kv_rows, rank)


def join_kernel(dp_count, *refs):
    parts, out = refs[:-1], refs[-1]
    width = parts[0].shape[2]
    here = lax.axis_index("dp")
    for step, part in enumerate(parts):
        out[:, :, pl.ds(pl.multiple_of((here ^ step) * width, lanes), width)] = part[...]


def vmem(count):
    return [pl.BlockSpec(memory_space=pltpu.VMEM)] * count


def smem(count):
    return [pl.BlockSpec(memory_space=pltpu.SMEM)] * count


def bits(count):
    return [1 << n for n in range(count.bit_length() - 1)]


def axis_count(axis):
    names = (axis,) if isinstance(axis, str) else axis
    return math.prod(lax.axis_size(name) for name in names)


def exchange(name, array, axis, bits):
    with jax.named_scope(name):
        return lax.ppermute(array, axis, xor_pairs(axis_count(axis), bits))


def xor_pairs(count, bits):
    return [(n, n ^ bits) for n in range(count)]


def on_device(inputs, grad_value, w_value, adapter_down, adapter_up, tenant_ids, slot_table):
    tokens, width = inputs.shape
    kv_width = grad_value.shape[1]
    own, rows, rank = adapter_down.shape
    kv_rows = adapter_up.shape[1]
    fsdp_count = lax.axis_size("fsdp")
    dp_count = lax.axis_size("dp")
    inner_count = 1
    while inner_count * inner_count < fsdp_count:
        inner_count *= 2
    layers = fsdp_count // inner_count
    split = 1
    while split * 2 <= dp_count and rows // (split * 2) >= lanes:
        split *= 2
    cols = rows // split
    tall = rows // lanes * rank + packed_rows(kv_rows)[0]

    down_t = adapter_down.transpose(0, 2, 1)
    downs, ups = [down_t], [adapter_up]
    for j in range(1, dp_count):
        downs.append(exchange("down_dp", down_t, "dp", j))
        ups.append(exchange("up_dp", adapter_up, "dp", j))
    with jax.named_scope("ids"):
        ids = lax.all_to_all(
            jnp.broadcast_to(tenant_ids[:, None, None], (fsdp_count, 1, lanes)), "fsdp", 0, 0, tiled=True
        )[:, 0, 0]

    w_here = lax.dynamic_slice_in_dim(w_value, lax.axis_index("dp") % split * cols, cols, 0)
    ws = [w_here] + [None] * (layers - 1)
    for bit in bits(layers):
        ws[bit] = exchange("w_layers", w_here, "fsdp", bit * inner_count)
    rels = [(i, 0) for i in range(0, inner_count, 2)]
    beside = jnp.concatenate([grad_value, w_here], axis=0)
    near = [exchange("g_w_layer", beside, "fsdp", i) for i, _ in rels[1:]]
    ids, downs, ups, ws, near = lax.optimization_barrier((ids, downs, ups, ws, near))
    held = jnp.concatenate([grad_value] + [n[:tokens] for n in near], axis=0)
    others = [exchange("g_dp", held, "dp", d) for d in range(1, split)]
    rels = rels + [(i, d) for d in range(1, split) for i, _ in rels]

    box = jax.ShapeDtypeStruct((fsdp_count, tall, lanes), BF16)
    box_bytes = 2 * fsdp_count * tall * lanes
    slots = jnp.sum(
        jnp.where(
            ids[:, None] == jnp.arange(slot_table.shape[0])[None, :], slot_table[None, :], 0
        ),
        axis=1,
    )
    ups[0] = pltpu.with_memory_space_constraint(ups[0], pltpu.HBM)
    downs[0] = pltpu.with_memory_space_constraint(downs[0], pltpu.HBM)
    sent = pl.pallas_call(
        functools.partial(select_kernel, dp_count),
        out_shape=pltpu.HBM(box.shape, BF16),
        in_specs=smem(1) + vmem(2 * dp_count),
        out_specs=pl.BlockSpec(memory_space=pltpu.HBM),
        scratch_shapes=[
            pltpu.VMEM(box.shape, BF16), pltpu.SemaphoreType.DMA((fsdp_count,)),
        ],
        compiler_params=params(),
        cost_estimate=cost(0, 2 * box_bytes),
        name="select",
    )(slots, *downs, *ups)
    with jax.named_scope("adapters_to_blocks"):
        got = lax.all_to_all(sent, "fsdp", 0, 0, tiled=True)
    for bit in reversed(bits(layers)):
        for k in range(0, layers, 2 * bit):
            if ws[k + bit] is None:
                ws[k + bit] = exchange("w_last", ws[k], "fsdp", bit * inner_count)
    ws = ws + [exchange("w_core", w, "fsdp", 1) for w in ws]
    near_other = [exchange("w_core", n, "fsdp", 1) for n in near]

    ws = [pltpu.with_memory_space_constraint(w, pltpu.HBM) for w in ws[:layers]] + ws[layers:]
    wide_cols = (2 * layers + 2 * len(near)) * cols
    pieces = pl.pallas_call(
        functools.partial(base_kernel, rels, len(near), layers),
        out_shape=[
            jax.ShapeDtypeStruct((tokens, wide_cols if i == 0 else (2 * layers - 2) * cols), BF16)
            for i, _ in rels
        ],
        in_specs=vmem(1 + 2 * len(near) + len(ws) + len(others)),
        out_specs=vmem(len(rels)),
        compiler_params=params(),
        cost_estimate=cost(
            base_weight * 2 * tokens * width * kv_width, base_weight * 4 * tokens * width
        ),
        name="base",
    )(grad_value, *near, *ws, *near_other, *others)
    pieces = [pieces[0]] + [
        exchange("pieces%d%d" % (i, d), p, ("fsdp", "dp"), i * dp_count + d)
        for (i, d), p in zip(rels[1:], pieces[1:])
    ]
    got, pieces[:-1] = lax.optimization_barrier((got, pieces[:-1]))

    tiles = rows // lanes
    halves = dp_count if tiles % dp_count == 0 else 1
    cut = tiles // halves * rank
    small = packed_rows(kv_rows)[0]
    back_shape = (fsdp_count * halves, cut + small, lanes)
    hidden, back = pl.pallas_call(
        functools.partial(middle_kernel, kv_rows, rank, halves),
        out_shape=[
            jax.ShapeDtypeStruct((tokens, rank), BF16),
            pltpu.HBM(back_shape, BF16),
        ],
        in_specs=vmem(3),
        out_specs=vmem(1) + [pl.BlockSpec(memory_space=pltpu.HBM)],
        scratch_shapes=[
            pltpu.VMEM((fsdp_count * halves, cut, lanes), BF16),
            pltpu.VMEM((fsdp_count * halves, small, lanes), BF16),
            pltpu.SemaphoreType.DMA((store_parts + 1,)),
        ],
        compiler_params=params(),
        cost_estimate=cost(4 * tokens * width * rank, 2 * tokens * width + 2 * box_bytes),
        name="middle",
    )(inputs, grad_value, got)
    with jax.named_scope("gradients_back"):
        axes = "fsdp" if halves == 1 else ("fsdp", "dp")
        returned = lax.all_to_all(back, axes, 0, 0, tiled=True)
    if halves > 1:
        all_slots = [slots] + [exchange("slots_dp", slots, "dp", j) for j in range(1, dp_count)]
        returned, all_slots = lax.optimization_barrier((returned, all_slots))
    returned, pieces = lax.optimization_barrier((returned, pieces))

    input_gradient_rows = pl.pallas_call(
        functools.partial(out_kernel, rels, layers, inner_count, split, rows, rank),
        out_shape=jax.ShapeDtypeStruct((tokens, width), BF16),
        in_specs=vmem(2 + len(rels)),
        out_specs=pl.BlockSpec(memory_space=pltpu.VMEM),
        compiler_params=params(),
        cost_estimate=cost(2 * tokens * width * rank, 4 * tokens * width + box_bytes),
        name="rows",
    )(hidden, got, *pieces)

    if halves > 1:
        part = (own, rank, rows // halves)

        def sum_halves(first, steps, extra, name):
            return pl.pallas_call(
                functools.partial(sum_halves_kernel, dp_count, kv_rows, first, steps),
                out_shape=[jax.ShapeDtypeStruct(shape, BF16) for shape in [part] * steps + extra],
                in_specs=smem(dp_count) + vmem(1),
                out_specs=vmem(steps + len(extra)),
                scratch_shapes=[pltpu.SMEM((dp_count, own * dp_count), jnp.int32)],
                compiler_params=params(),
                cost_estimate=cost(0, 2 * box_bytes),
                name=name,
            )(*all_slots, returned)

        *sums, grad_up = sum_halves(0, dp_count, [adapter_up.shape], "sum_all")
        received = [exchange("grads_dp", s, "dp", j) for j, s in enumerate(sums[1:], 1)]
        received, input_gradient_rows, sums[0], grad_up = lax.optimization_barrier(
            (received, input_gradient_rows, sums[0], grad_up)
        )
        grad_down_t = pl.pallas_call(
            functools.partial(join_kernel, dp_count),
            out_shape=jax.ShapeDtypeStruct((own, rank, rows), BF16),
            in_specs=vmem(dp_count),
            out_specs=pl.BlockSpec(memory_space=pltpu.VMEM),
            compiler_params=params(),
            cost_estimate=cost(0, 4 * own * rank * rows),
            name="join",
        )(sums[0], *received)
    else:
        sends = pl.pallas_call(
            functools.partial(sort_kernel, dp_count, own),
            out_shape=[jax.ShapeDtypeStruct((own, tall, lanes), BF16)] * (dp_count - 1),
            in_specs=smem(1) + vmem(1),
            out_specs=vmem(dp_count - 1),
            compiler_params=params(),
            cost_estimate=cost(0, 2 * box_bytes),
            name="sort",
        )(slots, returned)
        received = [
            exchange("grads_dp", s, "dp", j + 1) for j, s in enumerate(sends)
        ]
        received, input_gradient_rows = lax.optimization_barrier((received, input_gradient_rows))
        grad_down_t, grad_up = pl.pallas_call(
            functools.partial(sum_kernel, dp_count, kv_rows),
            out_shape=[
                jax.ShapeDtypeStruct((own, rank, rows), BF16),
                jax.ShapeDtypeStruct(adapter_up.shape, BF16),
            ],
            in_specs=smem(1) + vmem(dp_count),
            out_specs=vmem(2),
            compiler_params=params(),
            cost_estimate=cost(0, 2 * box_bytes),
            name="sums",
        )(slots, returned, *received)

    return (input_gradient_rows, grad_down_t.transpose(0, 2, 1), grad_up)


def solution(mesh):
    in_specs = (
        P(("fsdp", "dp"), None),
        P(("fsdp", "dp"), None),
        P("fsdp", None),
        P("dp", "fsdp", None),
        P("dp", "fsdp", None),
        P(("fsdp", "dp")),
        P(),
    )
    out_specs = (P(("fsdp", "dp"), None), P("dp", "fsdp", None), P("dp", "fsdp", None))
    return jax.shard_map(
        on_device, mesh=mesh, in_specs=in_specs, out_specs=out_specs, check_vma=False
    )
```
